256 devices in a mesh: dp: 2 (over x_lo), row: 8 (over x_hi, y), col: 16 (over z, core).
Axes of the slice: x: 4 (x_hi: 2, x_lo: 2; x = x_hi * 2 + x_lo), y: 4, z: 8, core: 2. Of those that a mesh axis runs over, the one named last changes fastest.
Arguments:
- tokens: bfloat16 [32768, 1024], P(('dp', 'row', 'col')), may hold values from -6 to 6
- out_grad: bfloat16 [32768, 1024], P(('dp', 'row', 'col')), may hold values from -3 to 3
- w_up: bfloat16 [1024, 4096], P('row', 'col'), may hold values from -0.1875 to 0.1875
- w_down: bfloat16 [4096, 1024], P('col', 'row'), may hold values from -0.09375 to 0.09375
Outputs:
- tokens_grad: bfloat16 [32768, 1024], P(('dp', 'row', 'col'))
- up_grad: bfloat16 [1024, 4096], P('row', 'col')
- down_grad: bfloat16 [4096, 1024], P('col', 'row')
The draws below stay inside these ranges and needn't reach their ends.
All inputs are finite; a program needn't handle non-finite values.
Results may differ from the reference program's by a relative error of at most 0.0049.
Values may be sent and summed in bfloat16 or wider, within the bound.
A program may use at most 64 MiB of HBM per device.

```python
import jax
import jax.numpy as jnp
from jax import lax

D = 1024
FF = 4096
TOKENS = 32768


def block_scale(own_key, shape, pieces, low, high):
    level = 1.0
    for axis_at, shards_of in pieces:
        heights = jax.random.uniform(jax.random.fold_in(jax.random.fold_in(own_key, 6), axis_at), (shards_of,), jnp.float32, low / len(pieces), high / len(pieces))
        level = level * jnp.repeat(jnp.exp(heights), shape[axis_at] // shards_of).reshape((-1,) + (1,) * (len(shape) - 1 - axis_at))
    return level


def scatter_about(rng, extent, spread, bound, split=(), kind=jnp.bfloat16):
    entries = jax.random.normal(rng, extent, jnp.float32) * spread
    if len(split) > 0:
        entries = block_scale(rng, extent, split, -0.22, 0.18) * entries
    return jnp.clip(entries, min=-bound, max=bound).astype(kind)


def setup_inputs(seed: int = 0) -> dict:
    key_list = jax.random.split(jax.random.key(seed), 5)
    tokens = scatter_about(key_list[0], (TOKENS, D), 1.0, 6.0, ((0, 256),))
    out_grad = scatter_about(key_list[1], (TOKENS, D), 0.5, 3.0, ((0, 256),))
    w_up = scatter_about(key_list[2], (D, FF), D ** -0.5, 0.1875, ((0, 8), (1, 16)))
    w_down = scatter_about(key_list[3], (FF, D), FF ** -0.5, 0.09375, ((0, 16), (1, 8)))
    return {"tokens": tokens, "out_grad": out_grad, "w_up": w_up, "w_down": w_down}


def gelu_tanh(value):
    return jax.nn.gelu(value, approximate=True)

def reference(tokens, out_grad, w_up, w_down):
    pre = jnp.dot(tokens, w_up, preferred_element_type=jnp.float32)
    hid_grad = lax.dot_general(out_grad, w_down, (((1,), (1,)), ((), ())), preferred_element_type=jnp.float32)
    hidden_f, pullback = jax.vjp(gelu_tanh, pre)
    pre_grad_f, = pullback(hid_grad)
    hidden = hidden_f.astype(jnp.bfloat16)
    pre_grad = pre_grad_f.astype(jnp.bfloat16)
    up_grad = lax.dot_general(tokens, pre_grad, (((0,), (0,)), ((), ())), preferred_element_type=jnp.float32)
    down_grad = lax.dot_general(hidden, out_grad, (((0,), (0,)), ((), ())), preferred_element_type=jnp.float32)
    tokens_grad = lax.dot_general(pre_grad, w_up, (((1,), (1,)), ((), ())), preferred_element_type=jnp.float32)
    return (tokens_grad.astype(jnp.bfloat16), up_grad.astype(jnp.bfloat16), down_grad.astype(jnp.bfloat16))
```

```python
import functools

import jax
import jax.numpy as jnp
from jax import lax
from jax.experimental import pallas as pl
from jax.experimental.pallas import tpu as pltpu
from jax.sharding import PartitionSpec as P

MESH = pl.DeviceIdType.MESH
BF16 = jnp.bfloat16
F32 = jnp.float32
NX, NY, NZ = 4, 4, 8


def gelu_pair(pre, hid_grad):
    k = 0.7978845608028654
    sq = pre * pre
    t = jnp.tanh(pre * (k + (k * 0.044715) * sq))
    half = 0.5 * (1.0 + t)
    hidden = pre * half
    slope = half + (0.5 * pre) * (1.0 - t * t) * (k + (3.0 * k * 0.044715) * sq)
    return hidden.astype(BF16), (hid_grad * slope).astype(BF16)


def kernel(
    tok, dy, wu, wd, dx_o, gu_o, gd_o,
    TOK, DY, W, WM, PG, HID, DWS, RX, SX, RZ, FS, FIN, DXS, DXC, DXY,
    ls, tks, tkr, dys, dyr, cts, ctr, cds, cdr, s1s, s1r, s2s, s2r, s3s, s3r, s3hs, s3hr,
    rxs, rxr, rzs, rzr, fs, fr, dcs, dcr, dvs, dvr,
):
    a = lax.axis_index("dp")
    row = lax.axis_index("row")
    col = lax.axis_index("col")
    xh, y = row // NY, row % NY
    z, c = col // 2, col % 2
    x = xh * 2 + a
    xr = [x, (x + 1) % NX, (x + 2) % NX, (x + 3) % NX]
    yr = [y, (y + 1) % NY, (y + 2) % NY, (y + 3) % NY]
    zr = [(z + k) % NZ for k in range(NZ)]

    def dev(x_, y_, z_, c_):
        return (x_ % 2, (x_ // 2) * NY + y_, z_ * 2 + c_)

    def send(src, dst, ss, rs, to):
        cp = pltpu.make_async_remote_copy(
            src_ref=src, dst_ref=dst, send_sem=ss, recv_sem=rs, device_id=to, device_id_type=MESH
        )
        cp.start()
        pending.append(cp)

    def arrived(ref, rs):
        pltpu.make_async_remote_copy(
            src_ref=ref, dst_ref=ref, send_sem=rs, recv_sem=rs, device_id=mate, device_id_type=MESH
        ).wait_recv()

    pending = []
    mate = dev(x, y, z, 1 - c)
    xo = xh * 2 + 1 - a
    peers = (
        [mate]
        + [dev(x, yr[k], z, c) for k in (1, 2, 3)]
        + [dev(xr[k], y, z, c) for k in (1, 2, 3)]
        + [dev(x, y, zr[k], c) for k in range(1, NZ)]
        + [dev(xo, yr[k], z, c) for k in (1, 2, 3)]
    )
    barrier = pltpu.get_barrier_semaphore()
    for p in peers:
        pl.semaphore_signal(barrier, inc=1, device_id=p, device_id_type=MESH)
    pl.semaphore_wait(barrier, len(peers))

    def block(ref, y_, c_):
        return ref.at[pl.ds(pl.multiple_of((c_ * NY + y_) * 128, 128), 128)]

    yp, ym = dev(x, yr[1], z, c), dev(x, yr[3], z, c)
    xp, xm = dev(xr[1], y, z, c), dev(xr[3], y, z, c)

    send(tok, block(TOK, y, c), tks.at[0], tkr.at[y], yp)
    send(dy, block(DY, y, c), dys.at[0], dyr.at[y], ym)
    send(dy, block(DY, y, c), dys.at[1], dyr.at[y], yp)
    send(tok, block(TOK, y, c), tks.at[1], tkr.at[y], ym)
    send(tok, block(TOK, y, c), cts.at[0], ctr.at[y], mate)
    send(dy, block(DY, y, c), cds.at[0], cdr.at[y], mate)
    own = [
        pltpu.make_async_copy(tok, block(TOK, y, c), ls.at[0]),
        pltpu.make_async_copy(dy, block(DY, y, c), ls.at[1]),
    ]
    for cp in own:
        cp.start()

    @pl.when(a == 0)
    def _():
        WM[...] = wu[...].T

    @pl.when(a == 1)
    def _():
        WM[...] = wd[...]

    def wpart(x_, z_, r0=0, rows=64):
        lanes = pl.ds(pl.multiple_of((x_ // 2) * 512, 512), 512)
        return W.at[x_ % 2, z_, pl.ds(r0, rows), lanes]

    def wblock(y_):
        lanes = pl.ds(pl.multiple_of(xh * 512 + y_ * 128, 128), 128)
        return W.at[a, z, :, lanes]

    def wm_rows(y_):
        return WM.at[pl.ds(pl.multiple_of(y_ * 64, 64), 64)]

    for k in (1, 2, 3):
        send(wm_rows(yr[k]), wblock(y), s1s.at[k], s1r.at[y], dev(x, yr[k], z, c))
    wblock(y)[...] = wm_rows(y)[...]
    for k in (1, 2, 3):
        arrived(wblock(yr[k]), s1r.at[yr[k]])
    for k in (1, 7, 2, 6, 3, 5, 4):
        send(wpart(x, z), wpart(x, z), s2s.at[k], s2r.at[z], dev(x, y, zr[k], c))

    def tok_relay():
        arrived(block(TOK, yr[3], c), tkr.at[yr[3]])
        send(block(TOK, yr[3], c), block(TOK, yr[3], c), tks.at[2], tkr.at[yr[3]], yp)
        send(block(TOK, yr[3], c), block(TOK, yr[3], c), cts.at[1], ctr.at[yr[3]], mate)
        arrived(block(DY, yr[1], c), dyr.at[yr[1]])
        send(block(DY, yr[1], c), block(DY, yr[1], c), dys.at[2], dyr.at[yr[1]], ym)
        send(block(DY, yr[1], c), block(DY, yr[1], c), cds.at[1], cdr.at[yr[1]], mate)

    def x_send(k):
        part = wpart(x, zr[k])
        send(part, part, s3s.at[0, k], s3r.at[x, zr[k]], xp)
        send(part, part, s3s.at[1, k], s3r.at[x, zr[k]], xm)

    def x_relay(k):
        arrived(wpart(xr[3], zr[k]), s3r.at[xr[3], zr[k]])
        part = wpart(xr[3], zr[k], 0, 32)
        send(part, part, s3hs.at[0, k], s3hr.at[0, zr[k]], xp)
        arrived(wpart(xr[1], zr[k]), s3r.at[xr[1], zr[k]])
        part = wpart(xr[1], zr[k], 32, 32)
        send(part, part, s3hs.at[1, k], s3hr.at[1, zr[k]], xm)

    order = (0, 1, 7, 2, 6, 3, 5, 4)
    for i, k in enumerate(order):
        if k:
            arrived(wpart(x, zr[k]), s2r.at[zr[k]])
        x_send(k)
        if i >= 2:
            x_relay(order[i - 2])
        if i == 5:
            tok_relay()
    for k in order[-2:]:
        x_relay(k)

    arrived(block(DY, yr[3], c), dyr.at[yr[3]])
    send(block(DY, yr[3], c), block(DY, yr[3], c), cds.at[2], cdr.at[yr[3]], mate)
    arrived(block(TOK, yr[1], c), tkr.at[yr[1]])
    send(block(TOK, yr[1], c), block(TOK, yr[1], c), cts.at[2], ctr.at[yr[1]], mate)
    arrived(block(TOK, yr[2], c), tkr.at[yr[2]])
    send(block(TOK, yr[2], c), block(TOK, yr[2], c), cts.at[3], ctr.at[yr[2]], mate)
    arrived(block(DY, yr[2], c), dyr.at[yr[2]])
    send(block(DY, yr[2], c), block(DY, yr[2], c), cds.at[3], cdr.at[yr[2]], mate)
    for k in order:
        arrived(wpart(xr[2], zr[k], 0, 32), s3hr.at[0, zr[k]])
        arrived(wpart(xr[2], zr[k], 32, 32), s3hr.at[1, zr[k]])
    for k in (0, 1, 3, 2):
        arrived(block(TOK, yr[k], 1 - c), ctr.at[yr[k]])
        arrived(block(DY, yr[k], 1 - c), cdr.at[yr[k]])
    for cp in own:
        cp.wait()

    nt = (((1,), (1,)), ((), ()))
    tn = (((0,), (0,)), ((), ()))
    nn = (((1,), (0,)), ((), ()))

    def dwpart(x_, g):
        lanes = pl.ds(pl.multiple_of((x_ // 2) * 512, 512), 512)
        return DWS.at[x_ % 2, pl.ds(4 * g, 4), :, lanes]

    def rxpart(x_, g):
        return RX.at[x_, pl.ds(4 * g, 4)]

    for g in (0, 1):
        cols = pl.ds(256 * g, 256)
        up = W[0, 4 * g : 4 * g + 4].reshape(256, 1024)
        down = W[1, 4 * g : 4 * g + 4].reshape(256, 1024)
        for b in range(4):
            rows = pl.ds(256 * b, 256)
            pre = lax.dot_general(TOK[rows, :], up, nt, preferred_element_type=F32)
            hg = lax.dot_general(DY[rows, :], down, nt, preferred_element_type=F32)
            hid, pg = gelu_pair(pre, hg)
            HID[rows, cols] = hid
            PG[rows, cols] = pg
        dwu = lax.dot_general(PG[:, cols], TOK[...], tn, preferred_element_type=F32)
        DWS[0, 4 * g : 4 * g + 4] = dwu.astype(BF16).reshape(4, 64, 1024)
        dwd = lax.dot_general(HID[:, cols], DY[...], tn, preferred_element_type=F32)
        DWS[1, 4 * g : 4 * g + 4] = dwd.astype(BF16).reshape(4, 64, 1024)
        for k in (2, 1, 3):
            send(dwpart(xr[k], g), rxpart(x, g), rxs.at[k, g], rxr.at[x, g], dev(xr[k], y, z, c))

    up = W[0].reshape(512, 1024)

    def crows(c_):
        return pl.ds(pl.multiple_of(c_ * 512, 512), 512)

    DXS[0] = lax.dot_general(PG[crows(1 - c), :], up, nn, preferred_element_type=F32).astype(BF16)
    send(DXS.at[0], DXC, dcs, dcr, mate)
    mine = lax.dot_general(PG[crows(c), :], up, nn, preferred_element_type=F32)
    arrived(DXC, dcr)
    DXS[1] = (mine + DXC[...].astype(F32)).astype(BF16)

    def dxrows(y_):
        return DXS.at[1, pl.ds(pl.multiple_of(y_ * 128, 128), 128)]

    for k in (2, 1, 3):
        send(dxrows(yr[k]), DXY.at[y], dvs.at[k], dvr.at[y], dev(x, yr[k], z, c))

    for g in (0, 1):
        total = dwpart(x, g)[...].astype(F32)
        for k in (1, 3, 2):
            arrived(rxpart(xr[k], g), rxr.at[xr[k], g])
            total = total + rxpart(xr[k], g)[...].astype(F32)
        SX[4 * g : 4 * g + 4] = total.astype(BF16)
    for k in (4, 3, 5, 2, 6, 1, 7):
        send(SX.at[zr[k]], RZ.at[z], rzs.at[k], rzr.at[z], dev(x, y, zr[k], c))

    total = dxrows(y)[...].astype(F32)
    for k in (1, 3, 2):
        arrived(DXY.at[yr[k]], dvr.at[yr[k]])
        total = total + DXY[yr[k]].astype(F32)
    dx_o[...] = total.astype(BF16)

    total = SX[z].astype(F32)
    for k in (1, 7, 2, 6, 3, 5, 4):
        arrived(RZ.at[zr[k]], rzr.at[zr[k]])
        total = total + RZ[zr[k]].astype(F32)
    total = total.astype(BF16)
    for i in range(NY):
        FS[i] = total[:, 128 * i : 128 * (i + 1)]

    def fin(a_, y_):
        return FIN.at[a_, pl.ds(pl.multiple_of(y_ * 64, 64), 64)]

    for k in (2, 1, 3):
        send(FS.at[yr[k]], fin(a, y), fs.at[0, k], fr.at[a, y], dev(x, yr[k], z, c))
    for k in (2, 1, 3, 0):
        send(FS.at[yr[k]], fin(a, y), fs.at[1, k], fr.at[a, y], dev(xo, yr[k], z, c))
    fin(a, y)[...] = FS[y]
    for k in (1, 3, 2):
        arrived(fin(a, yr[k]), fr.at[a, yr[k]])
    for k in (0, 1, 3, 2):
        arrived(fin(1 - a, yr[k]), fr.at[1 - a, yr[k]])
    gu_o[...] = FIN[0].T
    gd_o[...] = FIN[1]
    for cp in pending:
        cp.wait_send()


def shards(tokens, out_grad, w_up, w_down):
    vmem = pl.BlockSpec(memory_space=pltpu.VMEM)
    dma = pltpu.SemaphoreType.DMA
    return pl.pallas_call(
        kernel,
        out_shape=(
            jax.ShapeDtypeStruct((128, 1024), BF16),
            jax.ShapeDtypeStruct((128, 256), BF16),
            jax.ShapeDtypeStruct((256, 128), BF16),
        ),
        in_specs=[vmem] * 4,
        out_specs=(vmem,) * 3,
        scratch_shapes=[
            pltpu.VMEM((1024, 1024), BF16),
            pltpu.VMEM((1024, 1024), BF16),
            pltpu.VMEM((2, NZ, 64, 1024), BF16),
            pltpu.VMEM((256, 128), BF16),
            pltpu.VMEM((1024, 512), BF16),
            pltpu.VMEM((1024, 512), BF16),
            pltpu.VMEM((2, NZ, 64, 1024), BF16),
            pltpu.VMEM((NX, NZ, 64, 512), BF16),
            pltpu.VMEM((NZ, 64, 512), BF16),
            pltpu.VMEM((NZ, 64, 512), BF16),
            pltpu.VMEM((NY, 64, 128), BF16),
            pltpu.VMEM((2, 256, 128), BF16),
            pltpu.VMEM((2, 512, 1024), BF16),
            pltpu.VMEM((512, 1024), BF16),
            pltpu.VMEM((NY, 128, 1024), BF16),
            dma((2,)),
            dma((3,)), dma((NY,)), dma((3,)), dma((NY,)),
            dma((4,)), dma((NY,)), dma((4,)), dma((NY,)),
            dma((NY,)), dma((NY,)), dma((NZ,)), dma((NZ,)),
            dma((2, NZ)), dma((NX, NZ)), dma((2, NZ)), dma((2, NZ)),
            dma((NX, 2)), dma((NX, 2)), dma((NZ,)), dma((NZ,)),
            dma((2, NY)), dma((2, NY)),
            dma, dma, dma((NY,)), dma((NY,)),
        ],
        compiler_params=pltpu.CompilerParams(
            collective_id=0, has_side_effects=True, vmem_limit_bytes=56 << 20
        ),
        cost_estimate=pl.CostEstimate(
            flops=5 * 2 * 1024 * 512 * 1024, bytes_accessed=2 << 20, transcendentals=1024 * 512
        ),
        name="mlp_backward",
    )(tokens, out_grad, w_up, w_down)


def solution(mesh):
    return jax.shard_map(
        shards,
        mesh=mesh,
        in_specs=(
            P(("dp", "row", "col"), None),
            P(("dp", "row", "col"), None),
            P("row", "col"),
            P("col", "row"),
        ),
        out_specs=(P(("dp", "row", "col"), None), P("row", "col"), P("col", "row")),
        check_vma=False,
    )
```

```python
import functools

import jax
import jax.numpy as jnp
from jax import lax
from jax.experimental import pallas as pl
from jax.experimental.pallas import tpu as pltpu
from jax.sharding import PartitionSpec as P

MESH = pl.DeviceIdType.MESH
BF16 = jnp.bfloat16
F32 = jnp.float32
NX, NY, NZ = 4, 4, 8
ORDER = (4, 3, 5, 2, 6, 1, 7, 0)
POS = [ORDER.index(rel) for rel in range(NZ)]


def gelu_pair(pre, hid_grad):
    k = 0.7978845608028654
    sq = pre * pre
    t = jnp.tanh(pre * (k + (k * 0.044715) * sq))
    half = 0.5 * (1.0 + t)
    hidden = pre * half
    slope = half + (0.5 * pre) * (1.0 - t * t) * (k + (3.0 * k * 0.044715) * sq)
    return hidden.astype(BF16), (hid_grad * slope).astype(BF16)


def kernel(
    tok, dy, wu, wd, dx_o, gu_o, gd_o,
    TOK, DY, W, WM, PG, HID, DWS, RXA, RXB, RX, SR, SX, RZ, FS, FIN, DXS, DXC, DXY,
    ls, tks, tkr, dys, dyr, cts, ctr, cds, cdr, s1s, s1r, zps, zpr, zms, zmr, s3s, s3r, s3hs, s3hr,
    ras, rar, rbs, rbr, rds, rdr, rrs, rrr, rzs, rzr, fs, fr, dcs, dcr, dvs, dvr,
):
    a = lax.axis_index("dp")
    row = lax.axis_index("row")
    col = lax.axis_index("col")
    xh, y = row // NY, row % NY
    z, c = col // 2, col % 2
    x = xh * 2 + a
    xr = [x, (x + 1) % NX, (x + 2) % NX, (x + 3) % NX]
    yr = [y, (y + 1) % NY, (y + 2) % NY, (y + 3) % NY]
    zr = [(z + k) % NZ for k in range(NZ)]

    def dev(x_, y_, z_, c_):
        return (x_ % 2, (x_ // 2) * NY + y_, z_ * 2 + c_)

    def send(src, dst, ss, rs, to):
        cp = pltpu.make_async_remote_copy(
            src_ref=src, dst_ref=dst, send_sem=ss, recv_sem=rs, device_id=to, device_id_type=MESH
        )
        cp.start()
        pending.append(cp)

    def arrived(ref, rs):
        pltpu.make_async_remote_copy(
            src_ref=ref, dst_ref=ref, send_sem=rs, recv_sem=rs, device_id=mate, device_id_type=MESH
        ).wait_recv()

    pending = []
    mate = dev(x, y, z, 1 - c)
    yp, ym = dev(x, yr[1], z, c), dev(x, yr[3], z, c)
    xp, xm = dev(xr[1], y, z, c), dev(xr[3], y, z, c)
    zp, zm = dev(x, y, zr[1], c), dev(x, y, zr[7], c)
    xo = xh * 2 + 1 - a
    peers = (
        [mate]
        + [dev(x, yr[k], z, c) for k in (1, 2, 3)]
        + [dev(xr[k], y, z, c) for k in (1, 3)]
        + [dev(x, y, zr[k], c) for k in range(1, NZ)]
        + [dev(xo, yr[k], z, c) for k in (1, 2, 3)]
    )
    barrier = pltpu.get_barrier_semaphore()
    for p in peers:
        pl.semaphore_signal(barrier, inc=1, device_id=p, device_id_type=MESH)

    def block(ref, y_, c_):
        return ref.at[pl.ds(pl.multiple_of((c_ * NY + y_) * 128, 128), 128)]

    def lanes_of(x_):
        return pl.ds(pl.multiple_of((x_ // 2) * 512, 512), 512)

    def wpart(x_, rel, r0=0, rows=64):
        return W.at[x_ % 2, POS[rel], pl.ds(r0, rows), lanes_of(x_)]

    def wblock(y_):
        return W.at[a, POS[0], :, pl.ds(pl.multiple_of(xh * 512 + y_ * 128, 128), 128)]

    def wm_rows(y_):
        return WM.at[pl.ds(pl.multiple_of(y_ * 64, 64), 64)]

    own = [
        pltpu.make_async_copy(tok, block(TOK, y, c), ls.at[0]),
        pltpu.make_async_copy(dy, block(DY, y, c), ls.at[1]),
    ]
    for cp in own:
        cp.start()

    @pl.when(a == 0)
    def _():
        WM[...] = wu[...].T

    @pl.when(a == 1)
    def _():
        WM[...] = wd[...]

    wblock(y)[...] = wm_rows(y)[...]
    pl.semaphore_wait(barrier, len(peers))

    for k in (2, 1, 3):
        send(wm_rows(yr[k]), wblock(y), s1s.at[k], s1r.at[y], dev(x, yr[k], z, c))
    send(tok, block(TOK, y, c), tks.at[0], tkr.at[y], yp)
    send(dy, block(DY, y, c), dys.at[0], dyr.at[y], ym)
    send(dy, block(DY, y, c), dys.at[1], dyr.at[y], yp)
    send(tok, block(TOK, y, c), tks.at[1], tkr.at[y], ym)
    send(tok, block(TOK, y, c), cts.at[0], ctr.at[y], mate)
    send(dy, block(DY, y, c), cds.at[0], cdr.at[y], mate)

    def to_mate(k, t, d):
        if t:
            send(block(TOK, yr[k], c), block(TOK, yr[k], c), cts.at[k], ctr.at[yr[k]], mate)
        if d:
            send(block(DY, yr[k], c), block(DY, yr[k], c), cds.at[k], cdr.at[yr[k]], mate)

    def tok_relay():
        arrived(block(TOK, yr[3], c), tkr.at[yr[3]])
        send(block(TOK, yr[3], c), block(TOK, yr[3], c), tks.at[2], tkr.at[yr[3]], yp)
        arrived(block(DY, yr[1], c), dyr.at[yr[1]])
        send(block(DY, yr[1], c), block(DY, yr[1], c), dys.at[2], dyr.at[yr[1]], ym)
        to_mate(3, True, False)
        to_mate(1, False, True)

    def tok_second():
        arrived(block(DY, yr[3], c), dyr.at[yr[3]])
        to_mate(3, False, True)
        arrived(block(TOK, yr[1], c), tkr.at[yr[1]])
        to_mate(1, True, False)

    def tok_last():
        arrived(block(TOK, yr[2], c), tkr.at[yr[2]])
        to_mate(2, True, False)
        arrived(block(DY, yr[2], c), dyr.at[yr[2]])
        to_mate(2, False, True)

    def x_send(rel):
        part = wpart(x, rel)
        send(part, part, s3s.at[0, rel], s3r.at[0, rel], xp)
        send(part, part, s3s.at[1, rel], s3r.at[1, rel], xm)

    def x_relay(rel):
        arrived(wpart(xr[3], rel), s3r.at[0, rel])
        part = wpart(xr[3], rel, 0, 32)
        send(part, part, s3hs.at[0, rel], s3hr.at[0, rel], xp)
        arrived(wpart(xr[1], rel), s3r.at[1, rel])
        part = wpart(xr[1], rel, 32, 32)
        send(part, part, s3hs.at[1, rel], s3hr.at[1, rel], xm)

    def z_step(k):
        lo, hi = (8 - k) % 8, k
        if k == 4:
            arrived(wpart(x, 4, 0, 32), zpr.at[4])
            arrived(wpart(x, 4, 32, 32), zmr.at[4])
            x_send(4)
            return
        if k:
            arrived(wpart(x, lo), zpr.at[k])
        r0, rows = (0, 32) if k == 3 else (0, 64)
        send(wpart(x, lo, r0, rows), wpart(x, 7 - k, r0, rows), zps.at[k], zpr.at[k + 1], zp)
        if k:
            arrived(wpart(x, hi), zmr.at[k])
        r0, rows = (32, 32) if k == 3 else (0, 64)
        send(wpart(x, hi, r0, rows), wpart(x, k + 1, r0, rows), zms.at[k], zmr.at[k + 1], zm)
        x_send(lo)
        if k:
            x_send(hi)

    for k in (1, 3, 2):
        arrived(wblock(yr[k]), s1r.at[yr[k]])
    z_step(0)
    z_step(1)
    x_relay(0)
    tok_relay()
    z_step(2)
    x_relay(7)
    x_relay(1)
    z_step(3)
    tok_second()
    x_relay(6)
    z_step(4)
    x_relay(2)
    x_relay(5)
    x_relay(3)
    tok_last()
    x_relay(4)
    for k in (0, 1, 3, 2):
        arrived(block(TOK, yr[k], 1 - c), ctr.at[yr[k]])
        arrived(block(DY, yr[k], 1 - c), cdr.at[yr[k]])
    for rel in (0, 7, 1, 6, 2, 5, 3, 4):
        arrived(wpart(xr[2], rel, 0, 32), s3hr.at[0, rel])
        arrived(wpart(xr[2], rel, 32, 32), s3hr.at[1, rel])
    for cp in own:
        cp.wait()

    nt = (((1,), (1,)), ((), ()))
    tn = (((0,), (0,)), ((), ()))
    nn = (((1,), (0,)), ((), ()))

    def hidden_pass(g):
        cols = pl.ds(256 * g, 256)
        up = W[0, 4 * g : 4 * g + 4].reshape(256, 1024)
        down = W[1, 4 * g : 4 * g + 4].reshape(256, 1024)
        for b in range(4):
            rows = pl.ds(256 * b, 256)
            pre = lax.dot_general(TOK[rows, :], up, nt, preferred_element_type=F32)
            hg = lax.dot_general(DY[rows, :], down, nt, preferred_element_type=F32)
            hid, pg = gelu_pair(pre, hg)
            HID[rows, cols] = hid
            PG[rows, cols] = pg

    def weight_pass(g, i):
        cols = pl.ds(256 * g, 256)
        left, right = ((PG, TOK), (HID, DY))[i]
        grad = lax.dot_general(left[:, cols], right[...], tn, preferred_element_type=F32)
        DWS[i, 4 * g : 4 * g + 4] = grad.astype(BF16).reshape(4, 64, 1024)

    def piece(x_, p):
        return DWS.at[x_ % 2, p, :, lanes_of(x_)]

    def unit_send(u):
        pa, pb = 2 * u, 2 * u + 1
        send(piece(xr[2], pa), RXA.at[u], ras.at[u], rar.at[u], xp)
        send(piece(xr[2], pb), RXB.at[u], rbs.at[u], rbr.at[u], xm)
        send(piece(xr[1], pb), RX.at[0, pb], rds.at[0, u], rdr.at[0, u], xp)
        send(piece(xr[3], pa), RX.at[1, pa], rds.at[1, u], rdr.at[1, u], xm)

    def unit_relay(u):
        pa, pb = 2 * u, 2 * u + 1
        arrived(RXA.at[u], rar.at[u])
        SR[pa] = (piece(xr[1], pa)[...].astype(F32) + RXA[u].astype(F32)).astype(BF16)
        send(SR.at[pa], RX.at[0, pa], rrs.at[0, u], rrr.at[0, u], xp)
        arrived(RXB.at[u], rbr.at[u])
        SR[pb] = (piece(xr[3], pb)[...].astype(F32) + RXB[u].astype(F32)).astype(BF16)
        send(SR.at[pb], RX.at[1, pb], rrs.at[1, u], rrr.at[1, u], xm)

    def unit_sum(u):
        pa, pb = 2 * u, 2 * u + 1
        arrived(RX.at[1, pa], rdr.at[1, u])
        arrived(RX.at[0, pb], rdr.at[0, u])
        arrived(RX.at[0, pa], rrr.at[0, u])
        arrived(RX.at[1, pb], rrr.at[1, u])
        for p in (pa, pb):
            total = piece(x, p)[...].astype(F32) + RX[0, p].astype(F32) + RX[1, p].astype(F32)
            SX[p] = total.astype(BF16)
            rel = ORDER[p]
            if rel:
                send(SX.at[p], RZ.at[rel], rzs.at[rel], rzr.at[rel], dev(x, y, zr[rel], c))

    def crows(c_):
        return pl.ds(pl.multiple_of(c_ * 512, 512), 512)

    def dxrows(y_):
        return DXS.at[1, pl.ds(pl.multiple_of(y_ * 128, 128), 128)]

    hidden_pass(0)
    weight_pass(0, 0)
    weight_pass(0, 1)
    unit_send(0)
    unit_send(1)
    hidden_pass(1)
    weight_pass(1, 0)
    unit_relay(0)
    weight_pass(1, 1)
    unit_send(2)
    unit_send(3)
    unit_relay(1)
    up = W[0].reshape(512, 1024)
    DXS[0] = lax.dot_general(PG[crows(1 - c), :], up, nn, preferred_element_type=F32).astype(BF16)
    send(DXS.at[0], DXC, dcs, dcr, mate)
    mine = lax.dot_general(PG[crows(c), :], up, nn, preferred_element_type=F32)
    arrived(DXC, dcr)
    DXS[1] = (mine + DXC[...].astype(F32)).astype(BF16)
    for k in (2, 1, 3):
        send(dxrows(yr[k]), DXY.at[y], dvs.at[k], dvr.at[y], dev(x, yr[k], z, c))
    unit_sum(0)
    unit_relay(2)
    unit_sum(1)
    unit_relay(3)
    unit_sum(2)

    total = dxrows(y)[...].astype(F32)
    for k in (1, 3, 2):
        arrived(DXY.at[yr[k]], dvr.at[yr[k]])
        total = total + DXY[yr[k]].astype(F32)
    dx_o[...] = total.astype(BF16)

    unit_sum(3)
    total = SX[POS[0]].astype(F32)
    for k in (4, 3, 5, 2, 6, 1, 7):
        arrived(RZ.at[k], rzr.at[k])
        total = total + RZ[k].astype(F32)
    total = total.astype(BF16)
    for i in range(NY):
        FS[i] = total[:, 128 * i : 128 * (i + 1)]

    def fin(a_, y_):
        return FIN.at[a_, pl.ds(pl.multiple_of(y_ * 64, 64), 64)]

    for k in (2, 1, 3, 0):
        send(FS.at[yr[k]], fin(a, y), fs.at[1, k], fr.at[a, y], dev(xo, yr[k], z, c))
    for k in (2, 1, 3):
        send(FS.at[yr[k]], fin(a, y), fs.at[0, k], fr.at[a, y], dev(x, yr[k], z, c))
    fin(a, y)[...] = FS[y]
    for k in (1, 3, 2):
        arrived(fin(a, yr[k]), fr.at[a, yr[k]])
    for k in (0, 1, 3, 2):
        arrived(fin(1 - a, yr[k]), fr.at[1 - a, yr[k]])
    gu_o[...] = FIN[0].T
    gd_o[...] = FIN[1]
    for cp in pending:
        cp.wait_send()


def shards(tokens, out_grad, w_up, w_down):
    vmem = pl.BlockSpec(memory_space=pltpu.VMEM)
    dma = pltpu.SemaphoreType.DMA
    return pl.pallas_call(
        kernel,
        out_shape=(
            jax.ShapeDtypeStruct((128, 1024), BF16),
            jax.ShapeDtypeStruct((128, 256), BF16),
            jax.ShapeDtypeStruct((256, 128), BF16),
        ),
        in_specs=[vmem] * 4,
        out_specs=(vmem,) * 3,
        scratch_shapes=[
            pltpu.VMEM((1024, 1024), BF16),
            pltpu.VMEM((1024, 1024), BF16),
            pltpu.VMEM((2, NZ, 64, 1024), BF16),
            pltpu.VMEM((256, 128), BF16),
            pltpu.VMEM((1024, 512), BF16),
            pltpu.VMEM((1024, 512), BF16),
            pltpu.VMEM((2, NZ, 64, 1024), BF16),
            pltpu.VMEM((4, 64, 512), BF16),
            pltpu.VMEM((4, 64, 512), BF16),
            pltpu.VMEM((2, NZ, 64, 512), BF16),
            pltpu.VMEM((NZ, 64, 512), BF16),
            pltpu.VMEM((NZ, 64, 512), BF16),
            pltpu.VMEM((NZ, 64, 512), BF16),
            pltpu.VMEM((NY, 64, 128), BF16),
            pltpu.VMEM((2, 256, 128), BF16),
            pltpu.VMEM((2, 512, 1024), BF16),
            pltpu.VMEM((512, 1024), BF16),
            pltpu.VMEM((NY, 128, 1024), BF16),
            dma((2,)),
            dma((3,)), dma((NY,)), dma((3,)), dma((NY,)),
            dma((NY,)), dma((NY,)), dma((NY,)), dma((NY,)),
            dma((NY,)), dma((NY,)),
            dma((4,)), dma((5,)), dma((4,)), dma((5,)),
            dma((2, NZ)), dma((2, NZ)), dma((2, NZ)), dma((2, NZ)),
            dma((4,)), dma((4,)), dma((4,)), dma((4,)),
            dma((2, 4)), dma((2, 4)), dma((2, 4)), dma((2, 4)),
            dma((NZ,)), dma((NZ,)),
            dma((2, NY)), dma((2, NY)),
            dma, dma, dma((NY,)), dma((NY,)),
        ],
        compiler_params=pltpu.CompilerParams(
            collective_id=0, has_side_effects=True, vmem_limit_bytes=56 << 20
        ),
        cost_estimate=pl.CostEstimate(
            flops=5 * 2 * 1024 * 512 * 1024, bytes_accessed=2 << 20, transcendentals=1024 * 512
        ),
        name="mlp_backward",
    )(tokens, out_grad, w_up, w_down)


def solution(mesh):
    return jax.shard_map(
        shards,
        mesh=mesh,
        in_specs=(
            P(("dp", "row", "col"), None),
            P(("dp", "row", "col"), None),
            P("row", "col"),
            P("col", "row"),
        ),
        out_specs=(P(("dp", "row", "col"), None), P("row", "col"), P("col", "row")),
        check_vma=False,
    )
```

```python
import functools

import jax
import jax.numpy as jnp
from jax import lax
from jax.experimental import pallas as pl
from jax.experimental.pallas import tpu as pltpu
from jax.sharding import PartitionSpec as P

MESH = pl.DeviceIdType.MESH
BF16 = jnp.bfloat16
F32 = jnp.float32
NX, NY, NZ = 4, 4, 8
ORDER = (4, 3, 5, 2, 6, 1, 7, 0)
FULL = (0, 1, 7)
KPOS = (0, 1, 3, 2)
POS = [ORDER.index(rel) for rel in range(NZ)]


def gelu_pair(pre, hid_grad):
    k = 0.7978845608028654
    sq = pre * pre
    t = jnp.tanh(pre * (k + (k * 0.044715) * sq))
    half = 0.5 * (1.0 + t)
    hidden = pre * half
    slope = half + (0.5 * pre) * (1.0 - t * t) * (k + (3.0 * k * 0.044715) * sq)
    return hidden.astype(BF16), (hid_grad * slope).astype(BF16)


def kernel(
    tok, dy, wu, wd, dx_o, gw_o,
    TD, W, WU, WM, PH, DWS, RXA, RXB, RX, SR, SX, RZA, RZB, RZ, RF, SF, RC, SXF, RZF, FS, FIN, DXS, DXC, DXY,
    ls, tks, tkr, dys, dyr, cts, ctr, cds, cdr, s1s, s1r, zs, zrs, zfs, zfr,
    s3s, s3r, s3hs, s3hr, fcs, fcr, fms, fmr,
    ras, rar, rbs, rbr, rds, rdr, rrs, rrr, rfs, rfr, rcs, rcr, zas, zar, rzs, rzr, fs, fr, dcs, dcr, dvs, dvr,
):
    a = lax.axis_index("dp")
    row = lax.axis_index("row")
    col = lax.axis_index("col")
    xh, y = row // NY, row % NY
    z, c = col // 2, col % 2
    x = xh * 2 + a
    xr = [x, (x + 1) % NX, (x + 2) % NX, (x + 3) % NX]
    yr = [y, (y + 1) % NY, (y + 2) % NY, (y + 3) % NY]
    zr = [(z + k) % NZ for k in range(NZ)]
    TOK, DY = TD.at[0], TD.at[1]

    def dev(x_, y_, z_, c_):
        return (x_ % 2, (x_ // 2) * NY + y_, z_ * 2 + c_)

    def send(src, dst, ss, rs, to):
        cp = pltpu.make_async_remote_copy(
            src_ref=src, dst_ref=dst, send_sem=ss, recv_sem=rs, device_id=to, device_id_type=MESH
        )
        cp.start()
        pending.append(cp)

    def arrived(ref, rs):
        pltpu.make_async_remote_copy(
            src_ref=ref, dst_ref=ref, send_sem=rs, recv_sem=rs, device_id=mate, device_id_type=MESH
        ).wait_recv()

    pending = []
    mate = dev(x, y, z, 1 - c)
    yp, ym = dev(x, yr[1], z, c), dev(x, yr[3], z, c)
    xp, xm = dev(xr[1], y, z, c), dev(xr[3], y, z, c)
    zp, zm = dev(x, y, zr[1], c), dev(x, y, zr[7], c)
    xo = xh * 2 + 1 - a
    twin, across = dev(xo, y, z, c), dev(3 - x, y, z, c)
    peers = (
        [mate]
        + [dev(x, yr[k], z, c) for k in (1, 2, 3)]
        + [dev(xr[k], y, z, c) for k in (1, 3)]
        + [dev(x, y, zr[k], c) for k in range(1, NZ)]
        + [dev(xo, yr[k], z, c) for k in (1, 2, 3)]
    )
    barrier = pltpu.get_barrier_semaphore()
    for p in peers:
        pl.semaphore_signal(barrier, inc=1, device_id=p, device_id_type=MESH)

    def block(ref, k, o):
        return ref.at[pl.ds(o * 512 + KPOS[k] * 128, 128)]

    def half(h):
        return pl.ds(pl.multiple_of(h * 512, 512), 512)

    def wpart(x_, rel, r0=0, rows=64):
        return W.at[x_ % 2, POS[rel], pl.ds(r0, rows), half(x_ // 2)]

    def warr(i, h, rel):
        return W.at[i, POS[rel], :, half(h)]

    def wblock(y_):
        return W.at[:, POS[0], :, pl.ds(pl.multiple_of(xh * 512 + y_ * 128, 128), 128)]

    def wm_rows(y_):
        return WM.at[:, pl.ds(pl.multiple_of(y_ * 64, 64), 64)]

    own = [
        pltpu.make_async_copy(wu, WU, ls.at[0]),
        pltpu.make_async_copy(wd, WM.at[1], ls.at[1]),
        pltpu.make_async_copy(tok, block(TOK, 0, 0), ls.at[2]),
        pltpu.make_async_copy(dy, block(DY, 0, 0), ls.at[3]),
    ]
    for cp in own:
        cp.start()
    own[0].wait()
    WM[0] = WU[...].T
    own[1].wait()
    wblock(y)[...] = wm_rows(y)[...]
    own[2].wait()
    own[3].wait()
    pl.semaphore_wait(barrier, len(peers))

    for k in (2, 1, 3):
        send(wm_rows(yr[k]), wblock(y), s1s.at[k], s1r.at[y], dev(x, yr[k], z, c))
    tok0, dy0 = block(TOK, 0, 0), block(DY, 0, 0)
    send(tok0, block(TOK, 3, 0), tks.at[0], tkr.at[3], yp)
    send(dy0, block(DY, 1, 0), dys.at[0], dyr.at[1], ym)
    send(dy0, block(DY, 3, 0), dys.at[1], dyr.at[3], yp)
    send(tok0, block(TOK, 1, 0), tks.at[1], tkr.at[1], ym)

    def to_mate(k, t, d):
        if t:
            send(block(TOK, k, 0), block(TOK, k, 1), cts.at[k], ctr.at[k], mate)
        if d:
            send(block(DY, k, 0), block(DY, k, 1), cds.at[k], cdr.at[k], mate)

    def tok_relay():
        arrived(block(TOK, 3, 0), tkr.at[3])
        send(block(TOK, 3, 0), block(TOK, 2, 0), tks.at[2], tkr.at[2], yp)
        arrived(block(DY, 1, 0), dyr.at[1])
        send(block(DY, 1, 0), block(DY, 2, 0), dys.at[2], dyr.at[2], ym)
        to_mate(3, True, False)
        to_mate(1, False, True)

    def tok_second():
        arrived(block(DY, 3, 0), dyr.at[3])
        to_mate(3, False, True)
        arrived(block(TOK, 1, 0), tkr.at[1])
        to_mate(1, True, False)

    def tok_last():
        arrived(block(TOK, 2, 0), tkr.at[2])
        to_mate(2, True, False)
        arrived(block(DY, 2, 0), dyr.at[2])
        to_mate(2, False, True)

    def mate_done(*ks):
        for k in ks:
            arrived(block(TOK, k, 1), ctr.at[k])
            arrived(block(DY, k, 1), cdr.at[k])

    def x_send(rel):
        part = wpart(x, rel)
        if rel in FULL:
            send(part, part, fcs.at[rel], fcr.at[rel], across)
        else:
            send(part, part, s3s.at[0, rel], s3r.at[0, rel], xp)
            send(part, part, s3s.at[1, rel], s3r.at[1, rel], xm)

    def x_relay(rel):
        if rel in FULL:
            part = warr(1 - a, 1 - xh, rel)
            arrived(part, fcr.at[rel])
            send(part, part, fms.at[rel], fmr.at[rel], twin)
            return
        arrived(wpart(xr[3], rel), s3r.at[0, rel])
        part = wpart(xr[3], rel, 0, 32)
        send(part, part, s3hs.at[0, rel], s3hr.at[0, rel], xp)
        arrived(wpart(xr[1], rel), s3r.at[1, rel])
        part = wpart(xr[1], rel, 32, 32)
        send(part, part, s3hs.at[1, rel], s3hr.at[1, rel], xm)

    def x_done(rel):
        if rel in FULL:
            arrived(warr(a, 1 - xh, rel), fmr.at[rel])
        else:
            arrived(wpart(xr[2], rel, 0, 32), s3hr.at[0, rel])
            arrived(wpart(xr[2], rel, 32, 32), s3hr.at[1, rel])

    nt = (((1,), (1,)), ((), ()))
    tn = (((0,), (0,)), ((), ()))
    nn = (((1,), (0,)), ((), ()))

    def hidden_pass(g, *blocks):
        cols = pl.ds(256 * g, 256)
        up = W[0, 4 * g : 4 * g + 4].reshape(256, 1024)
        down = W[1, 4 * g : 4 * g + 4].reshape(256, 1024)
        for b in blocks:
            rows = pl.ds(256 * b, 256)
            pre = lax.dot_general(TOK[rows, :], up, nt, preferred_element_type=F32)
            hg = lax.dot_general(DY[rows, :], down, nt, preferred_element_type=F32)
            hid, pg = gelu_pair(pre, hg)
            PH[1, rows, cols] = hid
            PH[0, rows, cols] = pg

    def z_sends():
        for k in (1, 7, 2, 6):
            send(wpart(x, 0), wpart(x, 8 - k), zs.at[k], zrs.at[8 - k], dev(x, y, zr[k], c))
        other = warr(1 - a, xh, 0)
        send(other, warr(1 - a, xh, 7), zfs.at[0], zfr.at[0], zp)
        send(other, warr(1 - a, xh, 1), zfs.at[1], zfr.at[1], zm)

    def z_relay():
        arrived(wpart(x, 6), zrs.at[6])
        send(wpart(x, 6), wpart(x, 5), zs.at[5], zrs.at[5], zp)
        send(wpart(x, 6, 0, 32), wpart(x, 4, 0, 32), zs.at[4], zrs.at[4], dev(x, y, zr[2], c))
        arrived(wpart(x, 2), zrs.at[2])
        send(wpart(x, 2), wpart(x, 3), zs.at[3], zrs.at[3], zm)
        send(wpart(x, 2, 32, 32), wpart(x, 4, 32, 32), zs.at[0], zrs.at[0], dev(x, y, zr[6], c))
        x_send(6)
        x_send(2)

    def z_step(*rels):
        for rel in rels:
            arrived(wpart(x, rel), zrs.at[rel])
            x_send(rel)

    for k in (1, 3, 2):
        arrived(wblock(yr[k]), s1r.at[yr[k]])
    x_send(0)
    z_sends()
    to_mate(0, True, True)
    z_step(7, 1)
    x_relay(0)
    z_relay()
    tok_relay()
    x_relay(7)
    x_relay(1)
    z_step(5, 3)
    arrived(wpart(x, 4, 0, 32), zrs.at[4])
    arrived(wpart(x, 4, 32, 32), zrs.at[0])
    x_send(4)
    x_relay(6)
    x_relay(2)
    tok_second()
    x_relay(5)
    x_relay(3)
    arrived(warr(1 - a, xh, 7), zfr.at[0])
    arrived(warr(1 - a, xh, 1), zfr.at[1])
    for rel in (0, 7, 1, 6):
        x_done(rel)
    x_relay(4)
    mate_done(0, 1)
    hidden_pass(1, 0, 2)
    tok_last()
    for rel in (2, 5, 3, 4):
        x_done(rel)

    def weight_pass(g, i, h):
        left = PH[i, :, pl.ds(256 * g, 256)]
        grad = lax.dot_general(left, TD[i, :, half(h)], tn, preferred_element_type=F32)
        DWS[i, 4 * g : 4 * g + 4, :, half(h)] = grad.astype(BF16).reshape(4, 64, 512)

    def piece(x_, p, r0=0, rows=64):
        return DWS.at[x_ % 2, p, pl.ds(r0, rows), half(x_ // 2)]

    def add(*refs):
        total = refs[0][...].astype(F32)
        for ref in refs[1:]:
            total = total + ref[...].astype(F32)
        return total.astype(BF16)

    def far_send(p):
        send(piece(xr[2], p, 0, 32), RXA.at[p], ras.at[p], rar.at[p], xp)
        send(piece(xr[2], p, 32, 32), RXB.at[p], rbs.at[p], rbr.at[p], xm)

    def near_send(p):
        send(piece(xr[1], p, 32, 32), RX.at[0, p, pl.ds(32, 32)], rds.at[0, p], rdr.at[0, p], xp)
        send(piece(xr[3], p, 0, 32), RX.at[1, p, pl.ds(0, 32)], rds.at[1, p], rdr.at[1, p], xm)

    def x_pass(p):
        arrived(RXA.at[p], rar.at[p])
        SR[p, 0:32] = add(piece(xr[1], p, 0, 32), RXA.at[p])
        send(SR.at[p, pl.ds(0, 32)], RX.at[0, p, pl.ds(0, 32)], rrs.at[0, p], rrr.at[0, p], xp)
        arrived(RXB.at[p], rbr.at[p])
        SR[p, 32:64] = add(piece(xr[3], p, 32, 32), RXB.at[p])
        send(SR.at[p, pl.ds(32, 32)], RX.at[1, p, pl.ds(32, 32)], rrs.at[1, p], rrr.at[1, p], xm)

    def x_sum(p):
        arrived(RX.at[0, p, pl.ds(32, 32)], rdr.at[0, p])
        arrived(RX.at[1, p, pl.ds(0, 32)], rdr.at[1, p])
        arrived(RX.at[0, p, pl.ds(0, 32)], rrr.at[0, p])
        arrived(RX.at[1, p, pl.ds(32, 32)], rrr.at[1, p])
        SX[p] = add(piece(x, p), RX.at[0, p], RX.at[1, p])

    def z_far():
        send(SX.at[0, pl.ds(0, 32)], RZA.at[0], zas.at[0], zar.at[0], dev(x, y, zr[2], c))
        send(SX.at[0, pl.ds(32, 32)], RZA.at[1], zas.at[1], zar.at[1], dev(x, y, zr[6], c))
        send(SX.at[1], RZB.at[0], zas.at[2], zar.at[2], zp)
        send(SX.at[2], RZB.at[1], zas.at[3], zar.at[3], zm)

    def z_near(p):
        i = p - 3
        arrived(RZB.at[i], zar.at[2 + i])
        arrived(RZA.at[i], zar.at[i])
        own_rows, other_rows = pl.ds(32 * i, 32), pl.ds(32 - 32 * i, 32)
        SX[p, own_rows] = add(SX.at[p, own_rows], RZB.at[i, own_rows], RZA.at[i])
        SX[p, other_rows] = add(SX.at[p, other_rows], RZB.at[i, other_rows])
        rel = ORDER[p]
        send(SX.at[p], RZ.at[i], rzs.at[rel], rzr.at[rel], dev(x, y, zr[rel], c))

    def twin_send(p):
        send(DWS.at[a, p, :, half(1 - xh)], RF.at[p - 5], rfs.at[p - 5], rfr.at[p - 5], twin)

    def twin_pass(p):
        q = p - 5
        arrived(RF.at[q], rfr.at[q])
        SF[q] = add(DWS.at[1 - a, p, :, half(1 - xh)], RF.at[q])
        send(SF.at[q], RC.at[q], rcs.at[q], rcr.at[q], across)

    def full_sum(p):
        q = p - 5
        arrived(RC.at[q], rcr.at[q])
        SXF[q, a] = add(DWS.at[a, p, :, half(xh)], RC.at[q])
        SXF[q, 1 - a] = DWS[1 - a, p, :, half(xh)]
        rel = ORDER[p]
        if rel:
            send(SXF.at[q], RZF.at[q], rzs.at[rel], rzr.at[rel], dev(x, y, zr[rel], c))

    def dxrows(k):
        return DXS.at[1, pl.ds(KPOS[k] * 128, 128)]

    hidden_pass(0, 0, 2, 1)
    mate_done(3, 2)
    hidden_pass(0, 3)
    weight_pass(0, a, 1 - xh)
    for p in range(3):
        far_send(p)
    weight_pass(0, 1 - a, 1 - xh)
    weight_pass(0, 1 - a, xh)
    for p in range(3):
        near_send(p)
    weight_pass(0, a, xh)
    far_send(3)
    hidden_pass(1, 1)
    for p in range(3):
        x_pass(p)
    near_send(3)
    hidden_pass(1, 3)
    up = W[0].reshape(512, 1024)
    DXS[0] = lax.dot_general(PH[0, 512:1024], up, nn, preferred_element_type=F32).astype(BF16)
    send(DXS.at[0], DXC, dcs, dcr, mate)
    weight_pass(1, a, 1 - xh)
    far_send(4)
    weight_pass(1, 1 - a, 1 - xh)
    weight_pass(1, 1 - a, xh)
    near_send(4)
    x_pass(3)
    for p in (5, 6, 7):
        twin_send(p)
    mine = lax.dot_general(PH[0, 0:512], up, nn, preferred_element_type=F32)
    arrived(DXC, dcr)
    DXS[1] = (mine + DXC[...].astype(F32)).astype(BF16)
    for k in (2, 1, 3):
        send(dxrows(k), DXY.at[4 - k], dvs.at[k], dvr.at[4 - k], dev(x, yr[k], z, c))
    weight_pass(1, a, xh)
    x_pass(4)
    for p in (0, 1, 2):
        x_sum(p)
    z_far()
    twin_pass(5)
    twin_pass(6)
    x_sum(3)
    twin_pass(7)
    x_sum(4)
    z_near(3)
    z_near(4)
    full_sum(5)
    full_sum(6)

    for k in (1, 3, 2):
        arrived(DXY.at[k], dvr.at[k])
    dx_o[...] = add(dxrows(0), DXY.at[1], DXY.at[3], DXY.at[2])

    full_sum(7)
    for rel in (2, 6):
        arrived(RZ.at[POS[rel] - 3], rzr.at[rel])
    for rel in (1, 7):
        arrived(RZF.at[POS[rel] - 5], rzr.at[rel])
    total = [SXF[2, i].astype(F32) + RZF[0, i].astype(F32) + RZF[1, i].astype(F32) for i in (0, 1)]
    extra = RZ[0].astype(F32) + RZ[1].astype(F32)
    total[0] = (total[0] + jnp.where(a == 0, extra, 0.0)).astype(BF16)
    total[1] = (total[1] + jnp.where(a == 1, extra, 0.0)).astype(BF16)
    for j in range(NY):
        for i in (0, 1):
            FS[j, i] = total[i][:, 128 * j : 128 * (j + 1)]

    def fin(a_, y_):
        return FIN.at[a_, :, pl.ds(pl.multiple_of(y_ * 64, 64), 64)]

    for k in (2, 1, 3, 0):
        send(FS.at[yr[k]], fin(a, y), fs.at[1, k], fr.at[a, y], dev(xo, yr[k], z, c))
    for k in (2, 1, 3):
        send(FS.at[yr[k]], fin(a, y), fs.at[0, k], fr.at[a, y], dev(x, yr[k], z, c))
    fin(a, y)[...] = FS[y]
    for k in (1, 3, 2):
        arrived(fin(a, yr[k]), fr.at[a, yr[k]])
    for k in (0, 1, 3, 2):
        arrived(fin(1 - a, yr[k]), fr.at[1 - a, yr[k]])
    gw_o[...] = (FIN[0].astype(F32) + FIN[1].astype(F32)).astype(BF16)
    for cp in pending:
        cp.wait_send()


def finish(dx, gw, dx_o, gu_o, gd_o):
    dx_o[...] = dx[...]
    gu_o[...] = gw[0].T
    gd_o[...] = gw[1]


def shards(tokens, out_grad, w_up, w_down):
    vmem = pl.BlockSpec(memory_space=pltpu.VMEM)
    dma = pltpu.SemaphoreType.DMA
    dx, gw = pl.pallas_call(
        kernel,
        out_shape=(
            jax.ShapeDtypeStruct((128, 1024), BF16),
            jax.ShapeDtypeStruct((2, 256, 128), BF16),
        ),
        in_specs=[pl.BlockSpec(memory_space=pl.ANY)] * 4,
        out_specs=(vmem,) * 2,
        scratch_shapes=[
            pltpu.VMEM((2, 1024, 1024), BF16),
            pltpu.VMEM((2, NZ, 64, 1024), BF16),
            pltpu.VMEM((128, 256), BF16),
            pltpu.VMEM((2, 256, 128), BF16),
            pltpu.VMEM((2, 1024, 512), BF16),
            pltpu.VMEM((2, NZ, 64, 1024), BF16),
            pltpu.VMEM((5, 32, 512), BF16),
            pltpu.VMEM((5, 32, 512), BF16),
            pltpu.VMEM((2, 5, 64, 512), BF16),
            pltpu.VMEM((5, 64, 512), BF16),
            pltpu.VMEM((5, 64, 512), BF16),
            pltpu.VMEM((2, 32, 512), BF16),
            pltpu.VMEM((2, 64, 512), BF16),
            pltpu.VMEM((2, 64, 512), BF16),
            pltpu.VMEM((3, 64, 512), BF16),
            pltpu.VMEM((3, 64, 512), BF16),
            pltpu.VMEM((3, 64, 512), BF16),
            pltpu.VMEM((3, 2, 64, 512), BF16),
            pltpu.VMEM((2, 2, 64, 512), BF16),
            pltpu.VMEM((NY, 2, 64, 128), BF16),
            pltpu.VMEM((2, 2, 256, 128), BF16),
            pltpu.VMEM((2, 512, 1024), BF16),
            pltpu.VMEM((512, 1024), BF16),
            pltpu.VMEM((NY, 128, 1024), BF16),
            dma((4,)),
            dma((3,)), dma((NY,)), dma((3,)), dma((NY,)),
            dma((NY,)), dma((NY,)), dma((NY,)), dma((NY,)),
            dma((NY,)), dma((NY,)),
            dma((NZ,)), dma((NZ,)),
            dma((2,)), dma((2,)),
            dma((2, NZ)), dma((2, NZ)), dma((2, NZ)), dma((2, NZ)),
            dma((NZ,)), dma((NZ,)), dma((NZ,)), dma((NZ,)),
            dma((5,)), dma((5,)), dma((5,)), dma((5,)),
            dma((2, 5)), dma((2, 5)), dma((2, 5)), dma((2, 5)),
            dma((3,)), dma((3,)), dma((3,)), dma((3,)),
            dma((4,)), dma((4,)),
            dma((NZ,)), dma((NZ,)),
            dma((2, NY)), dma((2, NY)),
            dma, dma, dma((NY,)), dma((NY,)),
        ],
        compiler_params=pltpu.CompilerParams(
            collective_id=0, has_side_effects=True, vmem_limit_bytes=56 << 20
        ),
        cost_estimate=pl.CostEstimate(
            flops=5 * 2 * 1024 * 512 * 1024, bytes_accessed=2 << 20, transcendentals=1024 * 512
        ),
        name="mlp_backward",
    )(tokens, out_grad, w_up, w_down)
    return pl.pallas_call(
        finish,
        out_shape=(
            jax.ShapeDtypeStruct((128, 1024), BF16),
            jax.ShapeDtypeStruct((128, 256), BF16),
            jax.ShapeDtypeStruct((256, 128), BF16),
        ),
        in_specs=[vmem] * 2,
        out_specs=(vmem,) * 3,
        name="finish",
    )(dx, gw)


def solution(mesh):
    return jax.shard_map(
        shards,
        mesh=mesh,
        in_specs=(
            P(("dp", "row", "col"), None),
            P(("dp", "row", "col"), None),
            P("row", "col"),
            P("col", "row"),
        ),
        out_specs=(P(("dp", "row", "col"), None), P("row", "col"), P("col", "row")),
        check_vma=False,
    )
```

```python
import functools

import jax
import jax.numpy as jnp
from jax import lax
from jax.experimental import pallas as pl
from jax.experimental.pallas import tpu as pltpu
from jax.sharding import PartitionSpec as P

MESH = pl.DeviceIdType.MESH
BF16 = jnp.bfloat16
F32 = jnp.float32
NX, NY, NZ = 4, 4, 8
ORDER = (4, 3, 5, 2, 6, 1, 7, 0)
FULL = (0, 1, 7)
KPOS = (0, 1, 3, 2)
POS = [ORDER.index(rel) for rel in range(NZ)]


def gelu_pair(pre, hid_grad):
    k = 0.7978845608028654
    sq = pre * pre
    t = jnp.tanh(pre * (k + (k * 0.044715) * sq))
    half = 0.5 * (1.0 + t)
    hidden = pre * half
    slope = half + (0.5 * pre) * (1.0 - t * t) * (k + (3.0 * k * 0.044715) * sq)
    return hidden.astype(BF16), (hid_grad * slope).astype(BF16)


def kernel(
    tok, dy, wu, wd, dx_o, gw_o,
    TD, W, WU, WM, PH, DWS, RXA, RXB, RX, SR, SX, RZA, RZB, RZ, RF, SF, RC, SXF, RZF, FS, FIN, ACC, DXS, DXC, DXY,
    ls, tks, tkr, dys, dyr, cts, ctr, cds, cdr, s1s, s1r, zs, zrs, zfs, zfr,
    s3s, s3r, s3hs, s3hr, fcs, fcr, fms, fmr,
    ras, rar, rbs, rbr, rds, rdr, rrs, rrr, rfs, rfr, rcs, rcr, zas, zar, rzs, rzr, fs, fr, dcs, dcr, dvs, dvr,
):
    a = lax.axis_index("dp")
    row = lax.axis_index("row")
    col = lax.axis_index("col")
    xh, y = row // NY, row % NY
    z, c = col // 2, col % 2
    x = xh * 2 + a
    xr = [x, (x + 1) % NX, (x + 2) % NX, (x + 3) % NX]
    yr = [y, (y + 1) % NY, (y + 2) % NY, (y + 3) % NY]
    zr = [(z + k) % NZ for k in range(NZ)]
    TOK, DY = TD.at[0], TD.at[1]

    def dev(x_, y_, z_, c_):
        return (x_ % 2, (x_ // 2) * NY + y_, z_ * 2 + c_)

    def send(src, dst, ss, rs, to):
        cp = pltpu.make_async_remote_copy(
            src_ref=src, dst_ref=dst, send_sem=ss, recv_sem=rs, device_id=to, device_id_type=MESH
        )
        cp.start()
        pending.append(cp)

    def arrived(ref, rs):
        pltpu.make_async_remote_copy(
            src_ref=ref, dst_ref=ref, send_sem=rs, recv_sem=rs, device_id=mate, device_id_type=MESH
        ).wait_recv()

    pending = []
    mate = dev(x, y, z, 1 - c)
    yp, ym = dev(x, yr[1], z, c), dev(x, yr[3], z, c)
    xp, xm = dev(xr[1], y, z, c), dev(xr[3], y, z, c)
    zp, zm = dev(x, y, zr[1], c), dev(x, y, zr[7], c)
    xo = xh * 2 + 1 - a
    twin, across = dev(xo, y, z, c), dev(3 - x, y, z, c)
    peers = (
        [mate]
        + [dev(x, yr[k], z, c) for k in (1, 2, 3)]
        + [dev(xr[k], y, z, c) for k in (1, 3)]
        + [dev(x, y, zr[k], c) for k in range(1, NZ)]
        + [dev(xo, yr[k], z, c) for k in (1, 2, 3)]
    )
    barrier = pltpu.get_barrier_semaphore()
    for p in peers:
        pl.semaphore_signal(barrier, inc=1, device_id=p, device_id_type=MESH)

    def block(ref, k, o):
        return ref.at[pl.ds(o * 512 + KPOS[k] * 128, 128)]

    def half(h):
        return pl.ds(pl.multiple_of(h * 512, 512), 512)

    def wpart(x_, rel, r0=0, rows=64):
        return W.at[x_ % 2, POS[rel], pl.ds(r0, rows), half(x_ // 2)]

    def warr(i, h, rel):
        return W.at[i, POS[rel], :, half(h)]

    def wblock(y_):
        return W.at[:, POS[0], :, pl.ds(pl.multiple_of(xh * 512 + y_ * 128, 128), 128)]

    def wm_rows(y_):
        return WM.at[:, pl.ds(pl.multiple_of(y_ * 64, 64), 64)]

    own = [
        pltpu.make_async_copy(wu, WU, ls.at[0]),
        pltpu.make_async_copy(wd, WM.at[1], ls.at[1]),
        pltpu.make_async_copy(tok, block(TOK, 0, 0), ls.at[2]),
        pltpu.make_async_copy(dy, block(DY, 0, 0), ls.at[3]),
    ]
    for cp in own:
        cp.start()
    own[0].wait()
    WM[0] = WU[...].T
    own[1].wait()
    wblock(y)[...] = wm_rows(y)[...]
    own[2].wait()
    own[3].wait()
    pl.semaphore_wait(barrier, len(peers))

    def first_send():
        for k in (2, 1, 3):
            send(wm_rows(yr[k]), wblock(y), s1s.at[k], s1r.at[y], dev(x, yr[k], z, c))

    def first_done():
        for k in (1, 3, 2):
            arrived(wblock(yr[k]), s1r.at[yr[k]])

    tok0, dy0 = block(TOK, 0, 0), block(DY, 0, 0)

    def tok_up():
        send(tok0, block(TOK, 3, 0), tks.at[0], tkr.at[3], yp)

    def tok_down():
        send(tok0, block(TOK, 1, 0), tks.at[1], tkr.at[1], ym)

    def dy_up():
        send(dy0, block(DY, 3, 0), dys.at[1], dyr.at[3], yp)

    def dy_down():
        send(dy0, block(DY, 1, 0), dys.at[0], dyr.at[1], ym)

    def tok_done(k):
        arrived(block(TOK, k, 0), tkr.at[k])

    def dy_done(k):
        arrived(block(DY, k, 0), dyr.at[k])

    def tok_relay():
        tok_done(3)
        send(block(TOK, 3, 0), block(TOK, 2, 0), tks.at[2], tkr.at[2], yp)

    def dy_relay():
        dy_done(1)
        send(block(DY, 1, 0), block(DY, 2, 0), dys.at[2], dyr.at[2], ym)

    def tok_mate(k):
        send(block(TOK, k, 0), block(TOK, k, 1), cts.at[k], ctr.at[k], mate)

    def dy_mate(k):
        send(block(DY, k, 0), block(DY, k, 1), cds.at[k], cdr.at[k], mate)

    def mate_done(*ks):
        for k in ks:
            arrived(block(TOK, k, 1), ctr.at[k])
            arrived(block(DY, k, 1), cdr.at[k])

    def x_send(rel):
        part = wpart(x, rel)
        if rel in FULL:
            send(part, part, fcs.at[rel], fcr.at[rel], across)
        else:
            send(part, part, s3s.at[0, rel], s3r.at[0, rel], xp)
            send(part, part, s3s.at[1, rel], s3r.at[1, rel], xm)

    def x_relay(rel):
        part = warr(1 - a, 1 - xh, rel)
        arrived(part, fcr.at[rel])
        send(part, part, fms.at[rel], fmr.at[rel], twin)

    def x_up(rel):
        arrived(wpart(xr[3], rel), s3r.at[0, rel])
        part = wpart(xr[3], rel, 0, 32)
        send(part, part, s3hs.at[0, rel], s3hr.at[0, rel], xp)

    def x_down(rel):
        arrived(wpart(xr[1], rel), s3r.at[1, rel])
        part = wpart(xr[1], rel, 32, 32)
        send(part, part, s3hs.at[1, rel], s3hr.at[1, rel], xm)

    def x_done(rel):
        if rel in FULL:
            arrived(warr(a, 1 - xh, rel), fmr.at[rel])
            if rel:
                arrived(warr(1 - a, xh, rel), zfr.at[rel // 4])
        else:
            arrived(wpart(xr[2], rel, 0, 32), s3hr.at[0, rel])
            arrived(wpart(xr[2], rel, 32, 32), s3hr.at[1, rel])

    nt = (((1,), (1,)), ((), ()))
    tn = (((0,), (0,)), ((), ()))
    nn = (((1,), (0,)), ((), ()))

    def hidden_pass(g, *blocks):
        cols = pl.ds(256 * g, 256)
        up = W[0, 4 * g : 4 * g + 4].reshape(256, 1024)
        down = W[1, 4 * g : 4 * g + 4].reshape(256, 1024)
        for b in blocks:
            rows = pl.ds(256 * b, 256)
            pre = lax.dot_general(TOK[rows, :], up, nt, preferred_element_type=F32)
            hg = lax.dot_general(DY[rows, :], down, nt, preferred_element_type=F32)
            hid, pg = gelu_pair(pre, hg)
            PH[1, rows, cols] = hid
            PH[0, rows, cols] = pg

    def z_send(*ks):
        for k in ks:
            send(wpart(x, 0), wpart(x, 8 - k), zs.at[k], zrs.at[8 - k], dev(x, y, zr[k], c))

    def z_other():
        other = warr(1 - a, xh, 0)
        send(other, warr(1 - a, xh, 7), zfs.at[1], zfr.at[1], zp)
        send(other, warr(1 - a, xh, 1), zfs.at[0], zfr.at[0], zm)

    def z_done(rel):
        arrived(wpart(x, rel), zrs.at[rel])

    def z_done_4():
        arrived(wpart(x, 4, 0, 32), zrs.at[4])
        arrived(wpart(x, 4, 32, 32), zrs.at[0])

    def z_up():
        z_done(6)
        send(wpart(x, 6), wpart(x, 5), zs.at[5], zrs.at[5], zp)
        send(wpart(x, 6, 0, 32), wpart(x, 4, 0, 32), zs.at[4], zrs.at[4], dev(x, y, zr[2], c))

    def z_down():
        z_done(2)
        send(wpart(x, 2), wpart(x, 3), zs.at[3], zrs.at[3], zm)
        send(wpart(x, 2, 32, 32), wpart(x, 4, 32, 32), zs.at[0], zrs.at[0], dev(x, y, zr[6], c))

    def weight_pass(g, i, h):
        left = PH[i, :, pl.ds(256 * g, 256)]
        grad = lax.dot_general(left, TD[i, :, half(h)], tn, preferred_element_type=F32)
        DWS[i, 4 * g : 4 * g + 4, :, half(h)] = grad.astype(BF16).reshape(4, 64, 512)

    def piece(x_, p, r0=0, rows=64):
        return DWS.at[x_ % 2, p, pl.ds(r0, rows), half(x_ // 2)]

    def add(*refs):
        total = refs[0][...].astype(F32)
        for ref in refs[1:]:
            total = total + ref[...].astype(F32)
        return total.astype(BF16)

    def far_send(p):
        send(piece(xr[2], p, 0, 32), RXA.at[p], ras.at[p], rar.at[p], xp)
        send(piece(xr[2], p, 32, 32), RXB.at[p], rbs.at[p], rbr.at[p], xm)

    def near_send(p):
        send(piece(xr[1], p, 32, 32), RX.at[0, p, pl.ds(32, 32)], rds.at[0, p], rdr.at[0, p], xp)
        send(piece(xr[3], p, 0, 32), RX.at[1, p, pl.ds(0, 32)], rds.at[1, p], rdr.at[1, p], xm)

    def x_pass(p):
        arrived(RXA.at[p], rar.at[p])
        SR[p, 0:32] = add(piece(xr[1], p, 0, 32), RXA.at[p])
        send(SR.at[p, pl.ds(0, 32)], RX.at[0, p, pl.ds(0, 32)], rrs.at[0, p], rrr.at[0, p], xp)
        arrived(RXB.at[p], rbr.at[p])
        SR[p, 32:64] = add(piece(xr[3], p, 32, 32), RXB.at[p])
        send(SR.at[p, pl.ds(32, 32)], RX.at[1, p, pl.ds(32, 32)], rrs.at[1, p], rrr.at[1, p], xm)

    def x_sum(p):
        arrived(RX.at[0, p, pl.ds(32, 32)], rdr.at[0, p])
        arrived(RX.at[1, p, pl.ds(0, 32)], rdr.at[1, p])
        arrived(RX.at[0, p, pl.ds(0, 32)], rrr.at[0, p])
        arrived(RX.at[1, p, pl.ds(32, 32)], rrr.at[1, p])
        SX[p] = add(piece(x, p), RX.at[0, p], RX.at[1, p])

    def z_far_4():
        send(SX.at[0, pl.ds(0, 32)], RZA.at[0], zas.at[0], zar.at[0], dev(x, y, zr[2], c))
        send(SX.at[0, pl.ds(32, 32)], RZA.at[1], zas.at[1], zar.at[1], dev(x, y, zr[6], c))

    def z_far_up():
        send(SX.at[1], RZB.at[0], zas.at[2], zar.at[2], zp)

    def z_far_down():
        send(SX.at[2], RZB.at[1], zas.at[3], zar.at[3], zm)

    def z_near(p):
        i = p - 3
        arrived(RZB.at[i], zar.at[2 + i])
        arrived(RZA.at[i], zar.at[i])
        own_rows, other_rows = pl.ds(32 * i, 32), pl.ds(32 - 32 * i, 32)
        SX[p, own_rows] = add(SX.at[p, own_rows], RZB.at[i, own_rows], RZA.at[i])
        SX[p, other_rows] = add(SX.at[p, other_rows], RZB.at[i, other_rows])
        rel = ORDER[p]
        send(SX.at[p], RZ.at[i], rzs.at[rel], rzr.at[rel], dev(x, y, zr[rel], c))

    def twin_send(p):
        send(DWS.at[a, p, :, half(1 - xh)], RF.at[p - 5], rfs.at[p - 5], rfr.at[p - 5], twin)

    def twin_pass(p):
        q = p - 5
        arrived(RF.at[q], rfr.at[q])
        SF[q] = add(DWS.at[1 - a, p, :, half(1 - xh)], RF.at[q])
        send(SF.at[q], RC.at[q], rcs.at[q], rcr.at[q], across)

    def full_sum(p):
        q = p - 5
        arrived(RC.at[q], rcr.at[q])
        SXF[q, a] = add(DWS.at[a, p, :, half(xh)], RC.at[q])
        SXF[q, 1 - a] = DWS[1 - a, p, :, half(xh)]
        rel = ORDER[p]
        if rel:
            send(SXF.at[q], RZF.at[q], rzs.at[rel], rzr.at[rel], dev(x, y, zr[rel], c))

    def dxrows(k):
        return DXS.at[1, pl.ds(KPOS[k] * 128, 128)]

    up_all = W.at[0]

    def dx_mate():
        up = up_all[...].reshape(512, 1024)
        part = lax.dot_general(PH[0, 512:1024], up, nn, preferred_element_type=F32)
        DXS[0] = part.astype(BF16)
        send(DXS.at[0], DXC, dcs, dcr, mate)

    def dx_own():
        up = up_all[...].reshape(512, 1024)
        ACC[...] = lax.dot_general(PH[0, 0:512], up, nn, preferred_element_type=F32)

    def dx_send():
        for k in (2, 1, 3):
            send(dxrows(k), DXY.at[4 - k], dvs.at[k], dvr.at[4 - k], dev(x, yr[k], z, c))

    def dx_pair():
        arrived(DXC, dcr)
        DXS[1] = (ACC[...] + DXC[...].astype(F32)).astype(BF16)

    def dx_done():
        for k in (1, 3, 2):
            arrived(DXY.at[k], dvr.at[k])
        dx_o[...] = add(dxrows(0), DXY.at[1], DXY.at[3], DXY.at[2])

    def fin(a_, y_):
        return FIN.at[a_, :, pl.ds(pl.multiple_of(y_ * 64, 64), 64)]

    def total_send():
        for rel in (2, 6):
            arrived(RZ.at[POS[rel] - 3], rzr.at[rel])
        for rel in (1, 7):
            arrived(RZF.at[POS[rel] - 5], rzr.at[rel])
        total = [SXF[2, i].astype(F32) + RZF[0, i].astype(F32) + RZF[1, i].astype(F32) for i in (0, 1)]
        extra = RZ[0].astype(F32) + RZ[1].astype(F32)
        total[0] = (total[0] + jnp.where(a == 0, extra, 0.0)).astype(BF16)
        total[1] = (total[1] + jnp.where(a == 1, extra, 0.0)).astype(BF16)
        for j in range(NY):
            for i in (0, 1):
                FS[j, i] = total[i][:, 128 * j : 128 * (j + 1)]
        for k in (2, 1, 3, 0):
            send(FS.at[yr[k]], fin(a, y), fs.at[1, k], fr.at[a, y], dev(xo, yr[k], z, c))
        for k in (2, 1, 3):
            send(FS.at[yr[k]], fin(a, y), fs.at[0, k], fr.at[a, y], dev(x, yr[k], z, c))
        fin(a, y)[...] = FS[y]

    def total_done():
        for k in (1, 3, 2):
            arrived(fin(a, yr[k]), fr.at[a, yr[k]])
        for k in (0, 1, 3, 2):
            arrived(fin(1 - a, yr[k]), fr.at[1 - a, yr[k]])
        gw_o[...] = (FIN[0].astype(F32) + FIN[1].astype(F32)).astype(BF16)

    first_send()
    tok_up()
    dy_up()
    dy_down()
    tok_down()
    first_done()
    z_send(7)
    z_send(2)
    z_send(6)
    x_send(0)
    x_relay(0)
    z_done(1)
    x_send(1)
    z_up()
    z_send(1)
    x_send(6)
    tok_mate(0)
    dy_mate(0)
    z_down()
    dy_relay()
    x_send(2)
    tok_relay()
    z_done(5)
    x_send(5)
    x_up(6)
    dy_mate(1)
    z_done(3)
    x_send(3)
    z_done_4()
    x_send(4)
    x_up(2)
    z_done(7)
    x_send(7)
    tok_done(1)
    tok_mate(1)
    tok_mate(3)
    x_up(5)
    x_down(3)
    dy_done(3)
    dy_mate(3)
    z_other()
    x_up(3)
    x_down(2)
    x_done(0)
    x_down(4)
    x_up(4)
    x_down(5)
    x_relay(1)
    mate_done(0, 1)
    x_relay(7)
    x_down(6)
    x_done(3)
    x_done(2)
    tok_done(2)
    tok_mate(2)
    x_done(4)
    dy_done(2)
    dy_mate(2)
    x_done(5)
    hidden_pass(0, 2)
    hidden_pass(0, 1)
    hidden_pass(0, 0)
    mate_done(3, 2)
    hidden_pass(0, 3)
    weight_pass(0, a, 1 - xh)
    far_send(2)
    far_send(1)
    far_send(3)
    far_send(0)
    weight_pass(0, 1 - a, 1 - xh)
    x_done(7)
    weight_pass(0, 1 - a, xh)
    near_send(0)
    x_done(6)
    x_done(1)
    hidden_pass(1, 2)
    hidden_pass(1, 1)
    hidden_pass(1, 3)
    dx_mate()
    near_send(1)
    hidden_pass(1, 0)
    weight_pass(1, a, 1 - xh)
    twin_send(5)
    x_pass(1)
    twin_send(6)
    x_pass(0)
    x_pass(2)
    weight_pass(0, a, xh)
    near_send(2)
    weight_pass(1, a, xh)
    weight_pass(1, 1 - a, 1 - xh)
    dx_own()
    twin_pass(5)
    dx_pair()
    dx_send()
    x_sum(1)
    far_send(4)
    twin_pass(6)
    x_sum(0)
    z_far_up()
    z_far_4()
    x_pass(3)
    weight_pass(1, 1 - a, xh)
    near_send(4)
    x_sum(2)
    z_far_down()
    x_pass(4)
    near_send(3)
    full_sum(6)
    full_sum(5)
    twin_send(7)
    x_sum(4)
    z_near(4)
    x_sum(3)
    z_near(3)
    twin_pass(7)
    full_sum(7)
    total_send()
    dx_done()
    total_done()
    for cp in pending:
        cp.wait_send()


def finish(dx, gw, dx_o, gu_o, gd_o):
    dx_o[...] = dx[...]
    gu_o[...] = gw[0].T
    gd_o[...] = gw[1]


def shards(tokens, out_grad, w_up, w_down):
    vmem = pl.BlockSpec(memory_space=pltpu.VMEM)
    dma = pltpu.SemaphoreType.DMA
    dx, gw = pl.pallas_call(
        kernel,
        out_shape=(
            jax.ShapeDtypeStruct((128, 1024), BF16),
            jax.ShapeDtypeStruct((2, 256, 128), BF16),
        ),
        in_specs=[pl.BlockSpec(memory_space=pl.ANY)] * 4,
        out_specs=(vmem,) * 2,
        scratch_shapes=[
            pltpu.VMEM((2, 1024, 1024), BF16),
            pltpu.VMEM((2, NZ, 64, 1024), BF16),
            pltpu.VMEM((128, 256), BF16),
            pltpu.VMEM((2, 256, 128), BF16),
            pltpu.VMEM((2, 1024, 512), BF16),
            pltpu.VMEM((2, NZ, 64, 1024), BF16),
            pltpu.VMEM((5, 32, 512), BF16),
            pltpu.VMEM((5, 32, 512), BF16),
            pltpu.VMEM((2, 5, 64, 512), BF16),
            pltpu.VMEM((5, 64, 512), BF16),
            pltpu.VMEM((5, 64, 512), BF16),
            pltpu.VMEM((2, 32, 512), BF16),
            pltpu.VMEM((2, 64, 512), BF16),
            pltpu.VMEM((2, 64, 512), BF16),
            pltpu.VMEM((3, 64, 512), BF16),
            pltpu.VMEM((3, 64, 512), BF16),
            pltpu.VMEM((3, 64, 512), BF16),
            pltpu.VMEM((3, 2, 64, 512), BF16),
            pltpu.VMEM((2, 2, 64, 512), BF16),
            pltpu.VMEM((NY, 2, 64, 128), BF16),
            pltpu.VMEM((2, 2, 256, 128), BF16),
            pltpu.VMEM((512, 1024), F32),
            pltpu.VMEM((2, 512, 1024), BF16),
            pltpu.VMEM((512, 1024), BF16),
            pltpu.VMEM((NY, 128, 1024), BF16),
            dma((4,)),
            dma((3,)), dma((NY,)), dma((3,)), dma((NY,)),
            dma((NY,)), dma((NY,)), dma((NY,)), dma((NY,)),
            dma((NY,)), dma((NY,)),
            dma((NZ,)), dma((NZ,)),
            dma((2,)), dma((2,)),
            dma((2, NZ)), dma((2, NZ)), dma((2, NZ)), dma((2, NZ)),
            dma((NZ,)), dma((NZ,)), dma((NZ,)), dma((NZ,)),
            dma((5,)), dma((5,)), dma((5,)), dma((5,)),
            dma((2, 5)), dma((2, 5)), dma((2, 5)), dma((2, 5)),
            dma((3,)), dma((3,)), dma((3,)), dma((3,)),
            dma((4,)), dma((4,)),
            dma((NZ,)), dma((NZ,)),
            dma((2, NY)), dma((2, NY)),
            dma, dma, dma((NY,)), dma((NY,)),
        ],
        compiler_params=pltpu.CompilerParams(
            collective_id=0, has_side_effects=True, vmem_limit_bytes=56 << 20
        ),
        cost_estimate=pl.CostEstimate(
            flops=5 * 2 * 1024 * 512 * 1024, bytes_accessed=2 << 20, transcendentals=1024 * 512
        ),
        name="mlp_backward",
    )(tokens, out_grad, w_up, w_down)
    return pl.pallas_call(
        finish,
        out_shape=(
            jax.ShapeDtypeStruct((128, 1024), BF16),
            jax.ShapeDtypeStruct((128, 256), BF16),
            jax.ShapeDtypeStruct((256, 128), BF16),
        ),
        in_specs=[vmem] * 2,
        out_specs=(vmem,) * 3,
        name="finish",
    )(dx, gw)


def solution(mesh):
    return jax.shard_map(
        shards,
        mesh=mesh,
        in_specs=(
            P(("dp", "row", "col"), None),
            P(("dp", "row", "col"), None),
            P("row", "col"),
            P("col", "row"),
        ),
        out_specs=(P(("dp", "row", "col"), None), P("row", "col"), P("col", "row")),
        check_vma=False,
    )
```

```python
import functools

import jax
import jax.numpy as jnp
from jax import lax
from jax.experimental import pallas as pl
from jax.experimental.pallas import tpu as pltpu
from jax.sharding import PartitionSpec as P

MESH = pl.DeviceIdType.MESH
BF16 = jnp.bfloat16
F32 = jnp.float32
NX, NY, NZ = 4, 4, 8
ORDER = (4, 3, 5, 2, 6, 1, 7, 0)
KPOS = (0, 1, 3, 2)
POS = [ORDER.index(rel) for rel in range(NZ)]


def gelu_pair(pre, hid_grad):
    k = 0.7978845608028654
    sq = pre * pre
    t = jnp.tanh(pre * (k + (k * 0.044715) * sq))
    half = 0.5 * (1.0 + t)
    hidden = pre * half
    slope = half + (0.5 * pre) * (1.0 - t * t) * (k + (3.0 * k * 0.044715) * sq)
    return hidden.astype(BF16), (hid_grad * slope).astype(BF16)


def kernel(
    tok, dy, wu, wd, dx_o, gw_o,
    TD, W, WU, WM, PH, PT, DWS, RXA, RXB, RX, SR, SX, RZA, RZB, RZ, RF, SF, RC, SXF, RZF, RZO, FS, FIN, ACC, DXS, DXC, DXY,
    ls, tks, tkr, dys, dyr, cts, ctr, cds, cdr, s1s, s1r, zs, zrs,
    s3s, s3r, s3hs, s3hr,
    ras, rar, rbs, rbr, rds, rdr, rrs, rrr, rfs, rfr, rcs, rcr, zas, zar, rzs, rzr, ros, ror, fs, fr, dcs, dcr, dvs, dvr,
):
    a = lax.axis_index("dp")
    row = lax.axis_index("row")
    col = lax.axis_index("col")
    xh, y = row // NY, row % NY
    z, c = col // 2, col % 2
    x = xh * 2 + a
    xr = [x, (x + 1) % NX, (x + 2) % NX, (x + 3) % NX]
    yr = [y, (y + 1) % NY, (y + 2) % NY, (y + 3) % NY]
    zr = [(z + k) % NZ for k in range(NZ)]
    TOK, DY = TD.at[0], TD.at[1]

    def dev(x_, y_, z_, c_):
        return (x_ % 2, (x_ // 2) * NY + y_, z_ * 2 + c_)

    def send(src, dst, ss, rs, to):
        cp = pltpu.make_async_remote_copy(
            src_ref=src, dst_ref=dst, send_sem=ss, recv_sem=rs, device_id=to, device_id_type=MESH
        )
        cp.start()
        pending.append(cp)

    def arrived(ref, rs):
        pltpu.make_async_remote_copy(
            src_ref=ref, dst_ref=ref, send_sem=rs, recv_sem=rs, device_id=mate, device_id_type=MESH
        ).wait_recv()

    pending = []
    mate = dev(x, y, z, 1 - c)
    yp, ym = dev(x, yr[1], z, c), dev(x, yr[3], z, c)
    xp, xm = dev(xr[1], y, z, c), dev(xr[3], y, z, c)
    zp, zm = dev(x, y, zr[1], c), dev(x, y, zr[7], c)
    xo = xh * 2 + 1 - a
    twin, across = dev(xo, y, z, c), dev(3 - x, y, z, c)
    peers = (
        [mate]
        + [dev(x, yr[k], z, c) for k in (1, 2, 3)]
        + [dev(xr[k], y, z, c) for k in (1, 3)]
        + [dev(x, y, zr[k], c) for k in range(1, NZ)]
        + [dev(xo, yr[k], z, c) for k in (1, 2, 3)]
    )
    barrier = pltpu.get_barrier_semaphore()
    for p in peers:
        pl.semaphore_signal(barrier, inc=1, device_id=p, device_id_type=MESH)

    def block(ref, k, o):
        return ref.at[pl.ds(o * 512 + KPOS[k] * 128, 128)]

    def half(h):
        return pl.ds(pl.multiple_of(h * 512, 512), 512)

    def wpart(x_, rel, r0=0, rows=64):
        return W.at[x_ % 2, POS[rel], pl.ds(r0, rows), half(x_ // 2)]

    def wblock(y_):
        return W.at[a, POS[0], :, pl.ds(pl.multiple_of(xh * 512 + y_ * 128, 128), 128)]

    def wm_rows(y_):
        return WM.at[pl.ds(pl.multiple_of(y_ * 64, 64), 64)]

    own = [
        pltpu.make_async_copy(wu, WU, ls.at[0]),
        pltpu.make_async_copy(wd, WM, ls.at[1]),
        pltpu.make_async_copy(tok, block(TOK, 0, 0), ls.at[2]),
        pltpu.make_async_copy(dy, block(DY, 0, 0), ls.at[3]),
    ]
    for cp in own:
        cp.start()
    own[0].wait()
    own[1].wait()

    @pl.when(a == 0)
    def _():
        WM[...] = WU[...].T

    wblock(y)[...] = wm_rows(y)[...]
    own[2].wait()
    own[3].wait()
    pl.semaphore_wait(barrier, len(peers))

    def first_send():
        for k in (2, 1, 3):
            send(wm_rows(yr[k]), wblock(y), s1s.at[k], s1r.at[y], dev(x, yr[k], z, c))

    def first_done():
        for k in (1, 3, 2):
            arrived(wblock(yr[k]), s1r.at[yr[k]])

    tok0, dy0 = block(TOK, 0, 0), block(DY, 0, 0)

    def tok_up():
        send(tok0, block(TOK, 3, 0), tks.at[0], tkr.at[3], yp)

    def tok_down():
        send(tok0, block(TOK, 1, 0), tks.at[1], tkr.at[1], ym)

    def dy_up():
        send(dy0, block(DY, 3, 0), dys.at[1], dyr.at[3], yp)

    def dy_down():
        send(dy0, block(DY, 1, 0), dys.at[0], dyr.at[1], ym)

    def tok_done(k):
        arrived(block(TOK, k, 0), tkr.at[k])

    def dy_done(k):
        arrived(block(DY, k, 0), dyr.at[k])

    def tok_relay():
        tok_done(3)
        send(block(TOK, 3, 0), block(TOK, 2, 0), tks.at[2], tkr.at[2], yp)

    def dy_relay():
        dy_done(1)
        send(block(DY, 1, 0), block(DY, 2, 0), dys.at[2], dyr.at[2], ym)

    def tok_mate(k):
        send(block(TOK, k, 0), block(TOK, k, 1), cts.at[k], ctr.at[k], mate)

    def dy_mate(k):
        send(block(DY, k, 0), block(DY, k, 1), cds.at[k], cdr.at[k], mate)

    def mate_done(*ks):
        for k in ks:
            arrived(block(TOK, k, 1), ctr.at[k])
            arrived(block(DY, k, 1), cdr.at[k])

    def x_send(rel):
        for i, (r0, to) in enumerate(((0, xp), (32, xm), (32, xp), (0, xm))):
            part = wpart(x, rel, r0, 32)
            send(part, part, s3s.at[i, rel], s3r.at[i, rel], to)

    def x_up(rel):
        part = wpart(xr[3], rel, 0, 32)
        arrived(part, s3r.at[0, rel])
        send(part, part, s3hs.at[0, rel], s3hr.at[0, rel], xp)

    def x_down(rel):
        part = wpart(xr[1], rel, 32, 32)
        arrived(part, s3r.at[1, rel])
        send(part, part, s3hs.at[1, rel], s3hr.at[1, rel], xm)

    def x_done(rel):
        arrived(wpart(xr[3], rel, 32, 32), s3r.at[2, rel])
        arrived(wpart(xr[1], rel, 0, 32), s3r.at[3, rel])
        arrived(wpart(xr[2], rel, 0, 32), s3hr.at[0, rel])
        arrived(wpart(xr[2], rel, 32, 32), s3hr.at[1, rel])

    nt = (((1,), (1,)), ((), ()))
    tn = (((0,), (0,)), ((), ()))
    nn = (((1,), (0,)), ((), ()))

    def hidden_pass(g, *blocks):
        cols = pl.ds(256 * g, 256)
        up = W[0, 4 * g : 4 * g + 4].reshape(256, 1024)
        down = W[1, 4 * g : 4 * g + 4].reshape(256, 1024)
        for b in blocks:
            rows = pl.ds(256 * b, 256)
            pre = lax.dot_general(TOK[rows, :], up, nt, preferred_element_type=F32)
            hg = lax.dot_general(DY[rows, :], down, nt, preferred_element_type=F32)
            hid, pg = gelu_pair(pre, hg)
            PT[1, cols, rows] = hid.T
            PT[0, cols, rows] = pg.T
            PH[0, rows, cols] = pg

    def z_send(*ks):
        for k in ks:
            send(wpart(x, 0), wpart(x, 8 - k), zs.at[k], zrs.at[8 - k], dev(x, y, zr[k], c))

    def z_done(rel):
        arrived(wpart(x, rel), zrs.at[rel])

    def z_done_4():
        arrived(wpart(x, 4, 0, 32), zrs.at[4])
        arrived(wpart(x, 4, 32, 32), zrs.at[0])

    def z_up():
        z_done(6)
        send(wpart(x, 6), wpart(x, 5), zs.at[5], zrs.at[5], zp)
        send(wpart(x, 6, 0, 32), wpart(x, 4, 0, 32), zs.at[4], zrs.at[4], dev(x, y, zr[2], c))

    def z_down():
        z_done(2)
        send(wpart(x, 2), wpart(x, 3), zs.at[3], zrs.at[3], zm)
        send(wpart(x, 2, 32, 32), wpart(x, 4, 32, 32), zs.at[0], zrs.at[0], dev(x, y, zr[6], c))

    def weight_pass(g, i, h):
        left = PT[i, pl.ds(256 * g, 256)]
        grad = lax.dot_general(left, TD[i, :, half(h)], nn, preferred_element_type=F32)
        DWS[i, 4 * g : 4 * g + 4, :, half(h)] = grad.astype(BF16).reshape(4, 64, 512)

    def piece(x_, p, r0=0, rows=64):
        return DWS.at[x_ % 2, p, pl.ds(r0, rows), half(x_ // 2)]

    def add(*refs):
        total = refs[0][...].astype(F32)
        for ref in refs[1:]:
            total = total + ref[...].astype(F32)
        return total.astype(BF16)

    def far_send(p):
        send(piece(xr[2], p, 0, 32), RXA.at[p], ras.at[p], rar.at[p], xp)
        send(piece(xr[2], p, 32, 32), RXB.at[p], rbs.at[p], rbr.at[p], xm)

    def near_send(p):
        send(piece(xr[1], p, 32, 32), RX.at[0, p, pl.ds(32, 32)], rds.at[0, p], rdr.at[0, p], xp)
        send(piece(xr[3], p, 0, 32), RX.at[1, p, pl.ds(0, 32)], rds.at[1, p], rdr.at[1, p], xm)

    def x_pass(p):
        arrived(RXA.at[p], rar.at[p])
        SR[p, 0:32] = add(piece(xr[1], p, 0, 32), RXA.at[p])
        send(SR.at[p, pl.ds(0, 32)], RX.at[0, p, pl.ds(0, 32)], rrs.at[0, p], rrr.at[0, p], xp)
        arrived(RXB.at[p], rbr.at[p])
        SR[p, 32:64] = add(piece(xr[3], p, 32, 32), RXB.at[p])
        send(SR.at[p, pl.ds(32, 32)], RX.at[1, p, pl.ds(32, 32)], rrs.at[1, p], rrr.at[1, p], xm)

    def x_sum(p):
        arrived(RX.at[0, p, pl.ds(32, 32)], rdr.at[0, p])
        arrived(RX.at[1, p, pl.ds(0, 32)], rdr.at[1, p])
        arrived(RX.at[0, p, pl.ds(0, 32)], rrr.at[0, p])
        arrived(RX.at[1, p, pl.ds(32, 32)], rrr.at[1, p])
        SX[p] = add(piece(x, p), RX.at[0, p], RX.at[1, p])

    def z_far_4():
        send(SX.at[0, pl.ds(0, 32)], RZA.at[0], zas.at[0], zar.at[0], dev(x, y, zr[2], c))
        send(SX.at[0, pl.ds(32, 32)], RZA.at[1], zas.at[1], zar.at[1], dev(x, y, zr[6], c))

    def z_far_up():
        send(SX.at[1], RZB.at[0], zas.at[2], zar.at[2], zp)

    def z_far_down():
        send(SX.at[2], RZB.at[1], zas.at[3], zar.at[3], zm)

    def z_near(p):
        i = p - 3
        arrived(RZB.at[i], zar.at[2 + i])
        arrived(RZA.at[i], zar.at[i])
        own_rows, other_rows = pl.ds(32 * i, 32), pl.ds(32 - 32 * i, 32)
        SX[p, own_rows] = add(SX.at[p, own_rows], RZB.at[i, own_rows], RZA.at[i])
        SX[p, other_rows] = add(SX.at[p, other_rows], RZB.at[i, other_rows])
        rel = ORDER[p]
        send(SX.at[p], RZ.at[i], rzs.at[rel], rzr.at[rel], dev(x, y, zr[rel], c))

    def twin_send(p):
        send(DWS.at[a, p, :, half(1 - xh)], RF.at[p - 5], rfs.at[p - 5], rfr.at[p - 5], twin)

    def twin_pass(p):
        q = p - 5
        arrived(RF.at[q], rfr.at[q])
        SF[q] = add(DWS.at[1 - a, p, :, half(1 - xh)], RF.at[q])
        send(SF.at[q], RC.at[q], rcs.at[q], rcr.at[q], across)

    def full_sum(p):
        q = p - 5
        arrived(RC.at[q], rcr.at[q])
        SXF[q] = add(DWS.at[a, p, :, half(xh)], RC.at[q])
        rel = ORDER[p]
        if rel:
            send(SXF.at[q], RZF.at[q], rzs.at[rel], rzr.at[rel], dev(x, y, zr[rel], c))

    def own_send():
        for i, to in ((0, zp), (1, zm)):
            send(DWS.at[1 - a, 5 + i, :, half(xh)], RZO.at[i], ros.at[i], ror.at[i], to)

    def dxrows(k):
        return DXS.at[1, pl.ds(KPOS[k] * 128, 128)]

    up_all = W.at[0]

    def dx_rows(i):
        return pl.ds(256 * i, 256)

    def dx_part(rows):
        up = up_all[...].reshape(512, 1024)
        return lax.dot_general(PH[0, rows], up, nn, preferred_element_type=F32)

    def dx_mate(i):
        DXS[0, dx_rows(i)] = dx_part(pl.ds(512 + 256 * i, 256)).astype(BF16)
        send(DXS.at[0, dx_rows(i)], DXC.at[dx_rows(i)], dcs.at[i], dcr.at[i], mate)

    def dx_own(i):
        ACC[dx_rows(i)] = dx_part(dx_rows(i))

    def dx_pair(i):
        arrived(DXC.at[dx_rows(i)], dcr.at[i])
        DXS[1, dx_rows(i)] = (ACC[dx_rows(i)] + DXC[dx_rows(i)].astype(F32)).astype(BF16)

    def dx_send(*ks):
        for k in ks:
            send(dxrows(k), DXY.at[4 - k], dvs.at[k], dvr.at[4 - k], dev(x, yr[k], z, c))

    def dx_done():
        for k in (1, 3, 2):
            arrived(DXY.at[k], dvr.at[k])
        DXS[1, 0:128] = add(dxrows(0), DXY.at[1], DXY.at[3], DXY.at[2])
        dx_copy.start()

    dx_copy = pltpu.make_async_copy(dxrows(0), dx_o, ls.at[4])

    def fin(a_, i, y_):
        return FIN.at[a_, i, pl.ds(pl.multiple_of(y_ * 64, 64), 64)]

    def to_owners(i, *refs):
        total = add(*refs)
        for j in range(NY):
            FS[i, j] = total[:, 128 * j : 128 * (j + 1)]
        for k in (2, 1, 3, 0):
            send(FS.at[i, yr[k]], fin(a, i, y), fs.at[1, i, k], fr.at[a, i, y], dev(xo, yr[k], z, c))
        for k in (2, 1, 3):
            send(FS.at[i, yr[k]], fin(a, i, y), fs.at[0, i, k], fr.at[a, i, y], dev(x, yr[k], z, c))
        fin(a, i, y)[...] = FS[i, y]

    def own_total():
        for i in (0, 1):
            arrived(RZO.at[i], ror.at[i])
        to_owners(1, DWS.at[1 - a, 7, :, half(xh)], RZO.at[0], RZO.at[1])

    def total_send():
        for rel in (2, 6):
            arrived(RZ.at[POS[rel] - 3], rzr.at[rel])
        for rel in (1, 7):
            arrived(RZF.at[POS[rel] - 5], rzr.at[rel])
        to_owners(0, SXF.at[2], RZF.at[0], RZF.at[1], RZ.at[0], RZ.at[1])

    def total_done():
        for i in (1, 0):
            for k in (1, 3, 2):
                arrived(fin(a, i, yr[k]), fr.at[a, i, yr[k]])
            for k in (0, 1, 3, 2):
                arrived(fin(1 - a, i, yr[k]), fr.at[1 - a, i, yr[k]])
        gw_o[0] = add(FIN.at[0, 0], FIN.at[1, 1])
        gw_o[1] = add(FIN.at[1, 0], FIN.at[0, 1])

    first_send()
    dy_down()
    tok_up()
    dy_up()
    first_done()
    z_send(2)
    z_send(7)
    x_send(0)
    tok_mate(0)
    dy_mate(0)
    z_send(6)
    x_up(0)
    x_down(0)
    z_send(1)
    tok_down()
    z_done(1)
    x_send(1)
    z_up()
    x_send(6)
    dy_relay()
    dy_mate(1)
    tok_relay()
    z_down()
    x_send(2)
    z_done(7)
    x_send(7)
    z_done(5)
    x_send(5)
    z_done(3)
    x_send(3)
    z_done_4()
    x_send(4)
    x_up(2)
    dy_done(3)
    dy_mate(3)
    x_done(0)
    x_down(5)
    x_down(2)
    x_up(5)
    tok_done(1)
    tok_mate(1)
    mate_done(0, 1)
    x_up(4)
    x_down(4)
    x_down(3)
    tok_mate(3)
    x_down(6)
    x_down(1)
    x_up(3)
    x_up(6)
    x_up(1)
    x_down(7)
    tok_done(2)
    tok_mate(2)
    dy_done(2)
    dy_mate(2)
    x_done(5)
    x_done(2)
    x_done(4)
    x_up(7)
    x_done(3)
    hidden_pass(0, 0)
    hidden_pass(0, 1)
    hidden_pass(0, 2)
    mate_done(3, 2)
    hidden_pass(0, 3)
    weight_pass(0, a, 1 - xh)
    far_send(0)
    far_send(2)
    far_send(3)
    x_done(7)
    x_done(6)
    far_send(1)
    x_done(1)
    hidden_pass(1, 1)
    hidden_pass(1, 0)
    hidden_pass(1, 2)
    hidden_pass(1, 3)
    weight_pass(1, a, 1 - xh)
    twin_send(6)
    weight_pass(0, 1 - a, 1 - xh)
    weight_pass(0, 1 - a, xh)
    near_send(0)
    x_pass(0)
    dx_mate(1)
    dx_mate(0)
    far_send(4)
    x_pass(2)
    x_pass(1)
    dx_own(1)
    dx_own(0)
    weight_pass(1, 1 - a, 1 - xh)
    near_send(1)
    near_send(2)
    twin_pass(6)
    weight_pass(1, 1 - a, xh)
    own_send()
    weight_pass(0, a, xh)
    x_sum(0)
    z_far_4()
    twin_send(5)
    near_send(3)
    x_pass(3)
    dx_pair(1)
    dx_send(2, 3)
    dx_pair(0)
    dx_send(1)
    x_sum(1)
    z_far_up()
    weight_pass(1, a, xh)
    near_send(4)
    x_pass(4)
    x_sum(2)
    twin_send(7)
    z_far_down()
    twin_pass(5)
    full_sum(6)
    own_total()
    x_sum(3)
    z_near(3)
    x_sum(4)
    z_near(4)
    twin_pass(7)
    full_sum(5)
    full_sum(7)
    total_send()
    dx_done()
    total_done()
    dx_copy.wait()
    for cp in pending:
        cp.wait_send()


def finish(dx, gw, dx_o, gu_o, gd_o):
    dx_o[...] = dx[...]
    gu_o[...] = gw[0].T
    gd_o[...] = gw[1]


def shards(tokens, out_grad, w_up, w_down):
    vmem = pl.BlockSpec(memory_space=pltpu.VMEM)
    dma = pltpu.SemaphoreType.DMA
    dx, gw = pl.pallas_call(
        kernel,
        out_shape=(
            jax.ShapeDtypeStruct((128, 1024), BF16),
            jax.ShapeDtypeStruct((2, 256, 128), BF16),
        ),
        in_specs=[pl.BlockSpec(memory_space=pl.ANY)] * 4,
        out_specs=(pl.BlockSpec(memory_space=pl.ANY), vmem),
        scratch_shapes=[
            pltpu.VMEM((2, 1024, 1024), BF16),
            pltpu.VMEM((2, NZ, 64, 1024), BF16),
            pltpu.VMEM((128, 256), BF16),
            pltpu.VMEM((256, 128), BF16),
            pltpu.VMEM((1, 1024, 512), BF16),
            pltpu.VMEM((2, 512, 1024), BF16),
            pltpu.VMEM((2, NZ, 64, 1024), BF16),
            pltpu.VMEM((5, 32, 512), BF16),
            pltpu.VMEM((5, 32, 512), BF16),
            pltpu.VMEM((2, 5, 64, 512), BF16),
            pltpu.VMEM((5, 64, 512), BF16),
            pltpu.VMEM((5, 64, 512), BF16),
            pltpu.VMEM((2, 32, 512), BF16),
            pltpu.VMEM((2, 64, 512), BF16),
            pltpu.VMEM((2, 64, 512), BF16),
            pltpu.VMEM((3, 64, 512), BF16),
            pltpu.VMEM((3, 64, 512), BF16),
            pltpu.VMEM((3, 64, 512), BF16),
            pltpu.VMEM((3, 64, 512), BF16),
            pltpu.VMEM((2, 64, 512), BF16),
            pltpu.VMEM((2, 64, 512), BF16),
            pltpu.VMEM((2, NY, 64, 128), BF16),
            pltpu.VMEM((2, 2, 256, 128), BF16),
            pltpu.VMEM((512, 1024), F32),
            pltpu.VMEM((2, 512, 1024), BF16),
            pltpu.VMEM((512, 1024), BF16),
            pltpu.VMEM((NY, 128, 1024), BF16),
            dma((5,)),
            dma((3,)), dma((NY,)), dma((3,)), dma((NY,)),
            dma((NY,)), dma((NY,)), dma((NY,)), dma((NY,)),
            dma((NY,)), dma((NY,)),
            dma((NZ,)), dma((NZ,)),
            dma((4, NZ)), dma((4, NZ)), dma((2, NZ)), dma((2, NZ)),
            dma((5,)), dma((5,)), dma((5,)), dma((5,)),
            dma((2, 5)), dma((2, 5)), dma((2, 5)), dma((2, 5)),
            dma((3,)), dma((3,)), dma((3,)), dma((3,)),
            dma((4,)), dma((4,)),
            dma((NZ,)), dma((NZ,)),
            dma((2,)), dma((2,)),
            dma((2, 2, NY)), dma((2, 2, NY)),
            dma((2,)), dma((2,)), dma((NY,)), dma((NY,)),
        ],
        compiler_params=pltpu.CompilerParams(
            collective_id=0, has_side_effects=True, vmem_limit_bytes=56 << 20
        ),
        cost_estimate=pl.CostEstimate(
            flops=5 * 2 * 1024 * 512 * 1024, bytes_accessed=2 << 20, transcendentals=1024 * 512
        ),
        name="mlp_backward",
    )(tokens, out_grad, w_up, w_down)
    return pl.pallas_call(
        finish,
        out_shape=(
            jax.ShapeDtypeStruct((128, 1024), BF16),
            jax.ShapeDtypeStruct((128, 256), BF16),
            jax.ShapeDtypeStruct((256, 128), BF16),
        ),
        in_specs=[vmem] * 2,
        out_specs=(vmem,) * 3,
        name="finish",
    )(dx, gw)


def solution(mesh):
    return jax.shard_map(
        shards,
        mesh=mesh,
        in_specs=(
            P(("dp", "row", "col"), None),
            P(("dp", "row", "col"), None),
            P("row", "col"),
            P("col", "row"),
        ),
        out_specs=(P(("dp", "row", "col"), None), P("row", "col"), P("col", "row")),
        check_vma=False,
    )
```

```python
import math

import jax
import jax.numpy as jnp
from jax import lax
from jax.experimental import pallas as pl
from jax.experimental.pallas import tpu as pltpu
from jax.sharding import PartitionSpec as P

MESH = pl.DeviceIdType.MESH
BF16 = jnp.bfloat16
F32 = jnp.float32
NX, NY, NZ = 4, 4, 8
ORDER = (4, 3, 5, 2, 6, 1, 7, 0)
KPOS = (0, 1, 3, 2)
POS = [ORDER.index(rel) for rel in range(NZ)]


def gelu_pair(pre, hid_grad):
    k = 0.7978845608028654
    sq = pre * pre
    t = jnp.tanh(pre * (k + (k * 0.044715) * sq))
    half = 0.5 * (1.0 + t)
    hidden = pre * half
    slope = half + (0.5 * pre) * (1.0 - t * t) * (k + (3.0 * k * 0.044715) * sq)
    return hidden.astype(BF16), (hid_grad * slope).astype(BF16)


def kernel(
    tok, dy, wu, wd, dx_o, gw_o,
    TD, W, WU, WM, PH, PT, DWS, RXA, RXB, RX, SR, SX, RZA, RZB, RZ, RF, SF, RC, SXF, RZF, RZO, FS, FIN, ACC, DXS, DXC, DXY,
    ls, out, s1r, tkr, dyr, mtr, zrs, s3r, xdr, rar, rbr, xsr, rfr, rcr, zar, rzr, ror, fr, dcr, dvr,
):
    a = lax.axis_index("dp")
    row = lax.axis_index("row")
    col = lax.axis_index("col")
    xh, y = row // NY, row % NY
    z, c = col // 2, col % 2
    x = xh * 2 + a
    xr = [x, (x + 1) % NX, (x + 2) % NX, (x + 3) % NX]
    yr = [y, (y + 1) % NY, (y + 2) % NY, (y + 3) % NY]
    zr = [(z + k) % NZ for k in range(NZ)]
    TOK, DY = TD.at[0], TD.at[1]

    def dev(x_, y_, z_, c_):
        return (x_ % 2, (x_ // 2) * NY + y_, z_ * 2 + c_)

    rows_sent = [0] * 5

    def send(src, dst, kind, rs, to):
        pltpu.make_async_remote_copy(
            src_ref=src, dst_ref=dst, send_sem=out.at[kind], recv_sem=rs, device_id=to, device_id_type=MESH
        ).start()
        rows_sent[kind] += math.prod(src.shape) // 1024

    def sent(kind):
        rows = rows_sent[kind]
        ref = TD.at[0, pl.ds(0, rows)] if rows <= 1024 else TD.at[:, pl.ds(0, rows // 2)]
        if rows % 16:
            ref = WM.at[pl.ds(0, 8 * rows)]
        pltpu.make_async_remote_copy(
            src_ref=ref, dst_ref=ref, send_sem=out.at[kind], recv_sem=out.at[kind], device_id=mate,
            device_id_type=MESH,
        ).wait_send()

    def arrived(ref, rs):
        pltpu.make_async_remote_copy(
            src_ref=ref, dst_ref=ref, send_sem=rs, recv_sem=rs, device_id=mate, device_id_type=MESH
        ).wait_recv()

    mate = dev(x, y, z, 1 - c)
    yp, ym = dev(x, yr[1], z, c), dev(x, yr[3], z, c)
    xp, xm = dev(xr[1], y, z, c), dev(xr[3], y, z, c)
    zp, zm = dev(x, y, zr[1], c), dev(x, y, zr[7], c)
    xo = xh * 2 + 1 - a
    twin, across = dev(xo, y, z, c), dev(3 - x, y, z, c)
    peers = (
        [mate]
        + [dev(x, yr[k], z, c) for k in (1, 2, 3)]
        + [dev(xr[k], y, z, c) for k in (1, 3)]
        + [dev(x, y, zr[k], c) for k in range(1, NZ)]
        + [dev(xo, yr[k], z, c) for k in (1, 2, 3)]
    )
    barrier = pltpu.get_barrier_semaphore()
    for p in peers:
        pl.semaphore_signal(barrier, inc=1, device_id=p, device_id_type=MESH)

    def block(ref, k, o):
        return ref.at[pl.ds(o * 512 + KPOS[k] * 128, 128)]

    def half(h):
        return pl.ds(pl.multiple_of(h * 512, 512), 512)

    def wpart(x_, rel, r0=0, rows=64):
        return W.at[x_ % 2, POS[rel], pl.ds(r0, rows), half(x_ // 2)]

    def wblock(y_):
        return W.at[a, POS[0], :, pl.ds(pl.multiple_of(xh * 512 + y_ * 128, 128), 128)]

    def wm_rows(y_):
        return WM.at[pl.ds(pl.multiple_of(y_ * 64, 64), 64)]

    own = [
        pltpu.make_async_copy(wu, WU, ls.at[0]),
        pltpu.make_async_copy(wd, WM, ls.at[1]),
        pltpu.make_async_copy(tok, block(TOK, 0, 0), ls.at[2]),
        pltpu.make_async_copy(dy, block(DY, 0, 0), ls.at[3]),
    ]
    for cp in own:
        cp.start()
    own[0].wait()
    own[1].wait()

    @pl.when(a == 0)
    def _():
        WM[...] = WU[...].T

    wblock(y)[...] = wm_rows(y)[...]
    pl.semaphore_wait(barrier, len(peers))

    def first_send():
        for k in (2, 1, 3):
            send(wm_rows(yr[k]), wblock(y), 4, s1r, dev(x, yr[k], z, c))

    def first_done():
        arrived(WM.at[pl.ds(0, 192)], s1r)

    tok0, dy0 = block(TOK, 0, 0), block(DY, 0, 0)

    def tok_up():
        send(tok0, block(TOK, 3, 0), 0, tkr.at[3], yp)

    def tok_down():
        send(tok0, block(TOK, 1, 0), 0, tkr.at[1], ym)

    def dy_up():
        send(dy0, block(DY, 3, 0), 0, dyr.at[3], yp)

    def dy_down():
        send(dy0, block(DY, 1, 0), 0, dyr.at[1], ym)

    def tok_done(k):
        arrived(block(TOK, k, 0), tkr.at[k])

    def dy_done(k):
        arrived(block(DY, k, 0), dyr.at[k])

    def tok_relay():
        tok_done(3)
        send(block(TOK, 3, 0), block(TOK, 2, 0), 0, tkr.at[2], yp)

    def dy_relay():
        dy_done(1)
        send(block(DY, 1, 0), block(DY, 2, 0), 0, dyr.at[2], ym)

    def tok_mate(k):
        send(block(TOK, k, 0), block(TOK, k, 1), 0, mtr.at[k // 2], mate)

    def dy_mate(k):
        send(block(DY, k, 0), block(DY, k, 1), 0, mtr.at[k // 2], mate)

    def mate_done(*ks):
        arrived(TD.at[:, pl.ds(0, 256)], mtr.at[ks[0] // 2])

    def x_send(rel):
        for i, (r0, to) in enumerate(((0, xp), (32, xm), (32, xp), (0, xm))):
            part = wpart(x, rel, r0, 32)
            send(part, part, 1, s3r.at[i, rel] if i < 2 else xdr.at[rel], to)

    def x_up(rel):
        part = wpart(xr[3], rel, 0, 32)
        arrived(part, s3r.at[0, rel])
        send(part, part, 1, xdr.at[rel], xp)

    def x_down(rel):
        part = wpart(xr[1], rel, 32, 32)
        arrived(part, s3r.at[1, rel])
        send(part, part, 1, xdr.at[rel], xm)

    def x_done(rel):
        arrived(W.at[0, POS[rel]], xdr.at[rel])

    nt = (((1,), (1,)), ((), ()))
    tn = (((0,), (0,)), ((), ()))
    nn = (((1,), (0,)), ((), ()))

    def hidden_pass(g, *blocks):
        cols = pl.ds(256 * g, 256)
        up = W[0, 4 * g : 4 * g + 4].reshape(256, 1024)
        down = W[1, 4 * g : 4 * g + 4].reshape(256, 1024)
        for b in blocks:
            rows = pl.ds(256 * b, 256)
            pre = lax.dot_general(TOK[rows, :], up, nt, preferred_element_type=F32)
            hg = lax.dot_general(DY[rows, :], down, nt, preferred_element_type=F32)
            hid, pg = gelu_pair(pre, hg)
            PT[1, cols, rows] = hid.T
            PT[0, cols, rows] = pg.T
            PH[0, rows, cols] = pg

    def z_send(*ks):
        for k in ks:
            send(wpart(x, 0), wpart(x, 8 - k), 1, zrs.at[8 - k], dev(x, y, zr[k], c))

    def z_done(rel):
        arrived(wpart(x, rel), zrs.at[rel])

    def z_done_4():
        arrived(wpart(x, 4), zrs.at[4])

    def z_up():
        z_done(6)
        send(wpart(x, 6), wpart(x, 5), 1, zrs.at[5], zp)
        send(wpart(x, 6, 0, 32), wpart(x, 4, 0, 32), 1, zrs.at[4], dev(x, y, zr[2], c))

    def z_down():
        z_done(2)
        send(wpart(x, 2), wpart(x, 3), 1, zrs.at[3], zm)
        send(wpart(x, 2, 32, 32), wpart(x, 4, 32, 32), 1, zrs.at[4], dev(x, y, zr[6], c))

    def weight_pass(g, i, h):
        left = PT[i, pl.ds(256 * g, 256)]
        grad = lax.dot_general(left, TD[i, :, half(h)], nn, preferred_element_type=F32)
        DWS[i, 4 * g : 4 * g + 4, :, half(h)] = grad.astype(BF16).reshape(4, 64, 512)

    def piece(x_, p, r0=0, rows=64):
        return DWS.at[x_ % 2, p, pl.ds(r0, rows), half(x_ // 2)]

    def add(*refs):
        total = refs[0][...].astype(F32)
        for ref in refs[1:]:
            total = total + ref[...].astype(F32)
        return total.astype(BF16)

    def far_send(p):
        send(piece(xr[2], p, 0, 32), RXA.at[p], 2, rar.at[p], xp)
        send(piece(xr[2], p, 32, 32), RXB.at[p], 2, rbr.at[p], xm)

    def near_send(p):
        send(piece(xr[1], p, 32, 32), RX.at[0, p, pl.ds(32, 32)], 2, xsr.at[p], xp)
        send(piece(xr[3], p, 0, 32), RX.at[1, p, pl.ds(0, 32)], 2, xsr.at[p], xm)

    def x_pass(p):
        arrived(RXA.at[p], rar.at[p])
        SR[p, 0:32] = add(piece(xr[1], p, 0, 32), RXA.at[p])
        send(SR.at[p, pl.ds(0, 32)], RX.at[0, p, pl.ds(0, 32)], 2, xsr.at[p], xp)
        arrived(RXB.at[p], rbr.at[p])
        SR[p, 32:64] = add(piece(xr[3], p, 32, 32), RXB.at[p])
        send(SR.at[p, pl.ds(32, 32)], RX.at[1, p, pl.ds(32, 32)], 2, xsr.at[p], xm)

    def x_sum(p):
        arrived(RX.at[:, p], xsr.at[p])
        SX[p] = add(piece(x, p), RX.at[0, p], RX.at[1, p])

    def z_far_4():
        send(SX.at[0, pl.ds(0, 32)], RZA.at[0], 2, zar.at[0], dev(x, y, zr[2], c))
        send(SX.at[0, pl.ds(32, 32)], RZA.at[1], 2, zar.at[1], dev(x, y, zr[6], c))

    def z_far_up():
        send(SX.at[1], RZB.at[0], 2, zar.at[0], zp)

    def z_far_down():
        send(SX.at[2], RZB.at[1], 2, zar.at[1], zm)

    def z_near(p):
        i = p - 3
        arrived(DXC.at[pl.ds(0, 48)], zar.at[i])
        own_rows, other_rows = pl.ds(32 * i, 32), pl.ds(32 - 32 * i, 32)
        SX[p, own_rows] = add(SX.at[p, own_rows], RZB.at[i, own_rows], RZA.at[i])
        SX[p, other_rows] = add(SX.at[p, other_rows], RZB.at[i, other_rows])
        rel = ORDER[p]
        send(SX.at[p], RZ.at[i], 2, rzr, dev(x, y, zr[rel], c))

    def twin_send(p):
        send(DWS.at[a, p, :, half(1 - xh)], RF.at[p - 5], 2, rfr.at[p - 5], twin)

    def twin_pass(p):
        q = p - 5
        arrived(RF.at[q], rfr.at[q])
        SF[q] = add(DWS.at[1 - a, p, :, half(1 - xh)], RF.at[q])
        send(SF.at[q], RC.at[q], 2, rcr.at[q], across)

    def full_sum(p):
        q = p - 5
        arrived(RC.at[q], rcr.at[q])
        SXF[q] = add(DWS.at[a, p, :, half(xh)], RC.at[q])
        rel = ORDER[p]
        if rel:
            send(SXF.at[q], RZF.at[q], 2, rzr, dev(x, y, zr[rel], c))

    def own_send():
        for i, to in ((0, zp), (1, zm)):
            send(DWS.at[1 - a, 5 + i, :, half(xh)], RZO.at[i], 2, ror, to)

    def dxrows(k):
        return DXS.at[1, pl.ds(KPOS[k] * 128, 128)]

    up_all = W.at[0]

    def dx_rows(i):
        return pl.ds(256 * i, 256)

    def dx_part(rows):
        up = up_all[...].reshape(512, 1024)
        return lax.dot_general(PH[0, rows], up, nn, preferred_element_type=F32)

    def dx_mate(i):
        DXS[0, dx_rows(i)] = dx_part(pl.ds(512 + 256 * i, 256)).astype(BF16)
        send(DXS.at[0, dx_rows(i)], DXC.at[dx_rows(i)], 3, dcr.at[i], mate)

    def dx_own(i):
        ACC[dx_rows(i)] = dx_part(dx_rows(i))

    def dx_pair(i):
        arrived(DXC.at[dx_rows(i)], dcr.at[i])
        DXS[1, dx_rows(i)] = (ACC[dx_rows(i)] + DXC[dx_rows(i)].astype(F32)).astype(BF16)

    def dx_send(*ks):
        for k in ks:
            send(dxrows(k), DXY.at[4 - k], 3, dvr, dev(x, yr[k], z, c))

    def dx_done():
        arrived(DXY.at[pl.ds(1, 3)], dvr)
        DXS[1, 0:128] = add(dxrows(0), DXY.at[1], DXY.at[3], DXY.at[2])
        dx_copy.start()

    dx_copy = pltpu.make_async_copy(dxrows(0), dx_o, ls.at[4])

    def fin(a_, i, y_):
        return FIN.at[a_, i, pl.ds(pl.multiple_of(y_ * 64, 64), 64)]

    def to_owners(i, *refs):
        total = add(*refs)
        for j in range(NY):
            FS[i, j] = total[:, 128 * j : 128 * (j + 1)]
        for k in (2, 1, 3, 0):
            send(FS.at[i, yr[k]], fin(a, i, y), 3, fr, dev(xo, yr[k], z, c))
        for k in (2, 1, 3):
            send(FS.at[i, yr[k]], fin(a, i, y), 3, fr, dev(x, yr[k], z, c))
        fin(a, i, y)[...] = FS[i, y]

    def own_total():
        arrived(RZO, ror)
        to_owners(1, DWS.at[1 - a, 7, :, half(xh)], RZO.at[0], RZO.at[1])

    def total_send():
        arrived(DXC.at[pl.ds(0, 128)], rzr)
        to_owners(0, SXF.at[2], RZF.at[0], RZF.at[1], RZ.at[0], RZ.at[1])

    def total_done():
        arrived(DXC.at[pl.ds(0, 112)], fr)
        gw_o[0] = add(FIN.at[0, 0], FIN.at[1, 1])
        gw_o[1] = add(FIN.at[1, 0], FIN.at[0, 1])

    first_send()
    own[2].wait()
    own[3].wait()
    tok_up()
    dy_up()
    dy_down()
    first_done()
    z_send(7)
    z_send(2)
    tok_down()
    x_send(0)
    z_send(6)
    z_done(1)
    x_send(1)
    z_up()
    x_send(6)
    dy_relay()
    tok_relay()
    z_down()
    x_send(2)
    z_send(1)
    dy_mate(1)
    z_done(5)
    x_send(5)
    z_done(3)
    x_send(3)
    z_done_4()
    x_send(4)
    x_up(5)
    x_down(5)
    x_down(2)
    x_up(3)
    dy_done(3)
    dy_mate(3)
    x_up(2)
    tok_mate(0)
    dy_mate(0)
    x_down(3)
    x_down(4)
    tok_mate(3)
    x_up(4)
    z_done(7)
    x_send(7)
    x_down(1)
    tok_done(1)
    tok_mate(1)
    dy_done(2)
    dy_mate(2)
    tok_done(2)
    tok_mate(2)
    mate_done(0, 1)
    x_up(6)
    x_down(6)
    x_up(1)
    x_up(0)
    x_done(3)
    x_done(5)
    x_done(2)
    x_down(0)
    x_done(4)
    hidden_pass(0, 1)
    hidden_pass(0, 0)
    x_down(7)
    x_up(7)
    mate_done(3, 2)
    hidden_pass(0, 3)
    hidden_pass(0, 2)
    weight_pass(0, a, 1 - xh)
    far_send(2)
    far_send(0)
    weight_pass(0, 1 - a, 1 - xh)
    far_send(1)
    x_done(6)
    x_done(0)
    x_done(1)
    weight_pass(0, 1 - a, xh)
    near_send(0)
    x_done(7)
    hidden_pass(1, 1)
    far_send(3)
    hidden_pass(1, 0)
    x_pass(2)
    near_send(1)
    hidden_pass(1, 2)
    x_pass(0)
    hidden_pass(1, 3)
    weight_pass(1, a, 1 - xh)
    weight_pass(1, 1 - a, xh)
    twin_send(5)
    own_send()
    far_send(4)
    weight_pass(1, 1 - a, 1 - xh)
    dx_mate(1)
    twin_send(6)
    x_pass(1)
    dx_mate(0)
    near_send(2)
    x_pass(3)
    dx_own(1)
    weight_pass(0, a, xh)
    x_sum(0)
    near_send(4)
    dx_own(0)
    z_far_4()
    dx_pair(0)
    dx_send(1)
    dx_pair(1)
    dx_send(2, 3)
    twin_pass(5)
    weight_pass(1, a, xh)
    near_send(3)
    twin_pass(6)
    x_pass(4)
    x_sum(1)
    z_far_up()
    x_sum(2)
    z_far_down()
    twin_send(7)
    own_total()
    full_sum(5)
    full_sum(6)
    x_sum(3)
    x_sum(4)
    z_near(3)
    z_near(4)
    twin_pass(7)
    full_sum(7)
    total_send()
    dx_done()
    total_done()
    dx_copy.wait()
    for kind in range(5):
        sent(kind)


def finish(dx, gw, dx_o, gu_o, gd_o):
    dx_o[...] = dx[...]
    gu_o[...] = gw[0].T
    gd_o[...] = gw[1]


def shards(tokens, out_grad, w_up, w_down):
    vmem = pl.BlockSpec(memory_space=pltpu.VMEM)
    dma = pltpu.SemaphoreType.DMA
    dx, gw = pl.pallas_call(
        kernel,
        out_shape=(
            jax.ShapeDtypeStruct((128, 1024), BF16),
            jax.ShapeDtypeStruct((2, 256, 128), BF16),
        ),
        in_specs=[pl.BlockSpec(memory_space=pl.ANY)] * 4,
        out_specs=(pl.BlockSpec(memory_space=pl.ANY), vmem),
        scratch_shapes=[
            pltpu.VMEM((2, 1024, 1024), BF16),
            pltpu.VMEM((2, NZ, 64, 1024), BF16),
            pltpu.VMEM((128, 256), BF16),
            pltpu.VMEM((256, 128), BF16),
            pltpu.VMEM((1, 1024, 512), BF16),
            pltpu.VMEM((2, 512, 1024), BF16),
            pltpu.VMEM((2, NZ, 64, 1024), BF16),
            pltpu.VMEM((5, 32, 512), BF16),
            pltpu.VMEM((5, 32, 512), BF16),
            pltpu.VMEM((2, 5, 64, 512), BF16),
            pltpu.VMEM((5, 64, 512), BF16),
            pltpu.VMEM((5, 64, 512), BF16),
            pltpu.VMEM((2, 32, 512), BF16),
            pltpu.VMEM((2, 64, 512), BF16),
            pltpu.VMEM((2, 64, 512), BF16),
            pltpu.VMEM((3, 64, 512), BF16),
            pltpu.VMEM((3, 64, 512), BF16),
            pltpu.VMEM((3, 64, 512), BF16),
            pltpu.VMEM((3, 64, 512), BF16),
            pltpu.VMEM((2, 64, 512), BF16),
            pltpu.VMEM((2, 64, 512), BF16),
            pltpu.VMEM((2, NY, 64, 128), BF16),
            pltpu.VMEM((2, 2, 256, 128), BF16),
            pltpu.VMEM((512, 1024), F32),
            pltpu.VMEM((2, 512, 1024), BF16),
            pltpu.VMEM((512, 1024), BF16),
            pltpu.VMEM((NY, 128, 1024), BF16),
            dma((5,)), dma((5,)), dma,
            dma((NY,)), dma((NY,)), dma((2,)),
            dma((NZ,)), dma((2, NZ)), dma((NZ,)),
            dma((5,)), dma((5,)), dma((5,)),
            dma((3,)), dma((3,)), dma((2,)), dma, dma, dma,
            dma((2,)), dma,
        ],
        compiler_params=pltpu.CompilerParams(
            collective_id=0, has_side_effects=True, vmem_limit_bytes=56 << 20
        ),
        cost_estimate=pl.CostEstimate(
            flops=5 * 2 * 1024 * 512 * 1024, bytes_accessed=2 << 20, transcendentals=1024 * 512
        ),
        name="mlp_backward",
    )(tokens, out_grad, w_up, w_down)
    return pl.pallas_call(
        finish,
        out_shape=(
            jax.ShapeDtypeStruct((128, 1024), BF16),
            jax.ShapeDtypeStruct((128, 256), BF16),
            jax.ShapeDtypeStruct((256, 128), BF16),
        ),
        in_specs=[vmem] * 2,
        out_specs=(vmem,) * 3,
        name="finish",
    )(dx, gw)


def solution(mesh):
    return jax.shard_map(
        shards,
        mesh=mesh,
        in_specs=(
            P(("dp", "row", "col"), None),
            P(("dp", "row", "col"), None),
            P("row", "col"),
            P("col", "row"),
        ),
        out_specs=(P(("dp", "row", "col"), None), P("row", "col"), P("col", "row")),
        check_vma=False,
    )
```

```python
import math

import jax
import jax.numpy as jnp
from jax import lax
from jax.experimental import pallas as pl
from jax.experimental.pallas import tpu as pltpu
from jax.sharding import PartitionSpec as P

MESH = pl.DeviceIdType.MESH
BF16 = jnp.bfloat16
F32 = jnp.float32
NX, NY, NZ = 4, 4, 8
ORDER = (4, 3, 5, 2, 6, 1, 7, 0)
KPOS = (0, 1, 3, 2)
POS = [ORDER.index(rel) for rel in range(NZ)]


def gelu_pair(pre, hid_grad):
    k = 0.7978845608028654
    sq = pre * pre
    t = jnp.tanh(pre * (k + (k * 0.044715) * sq))
    half = 0.5 * (1.0 + t)
    hidden = pre * half
    slope = half + (0.5 * pre) * (1.0 - t * t) * (k + (3.0 * k * 0.044715) * sq)
    return hidden.astype(BF16), (hid_grad * slope).astype(BF16)


def kernel(
    tok, dy, wu, wd, dx_o, gw_o,
    TD, W, WU, WM, PH, PT, DWS, RXA, RXB, RX, SR, SX, RZA, RZB, RZ, RF, SF, RC, SXF, RZF, RZO, FS, ACC, DXS, DXC, DXY,
    ls, out, s1r, tkr, dyr, mtr, zrs, s3r, xdr, rar, rbr, xsr, rfr, rcr, zar, rzr, ror, fr, dcr, dvr,
):
    a = lax.axis_index("dp")
    row = lax.axis_index("row")
    col = lax.axis_index("col")
    xh, y = row // NY, row % NY
    z, c = col // 2, col % 2
    x = xh * 2 + a
    xr = [x, (x + 1) % NX, (x + 2) % NX, (x + 3) % NX]
    yr = [y, (y + 1) % NY, (y + 2) % NY, (y + 3) % NY]
    zr = [(z + k) % NZ for k in range(NZ)]
    TOK, DY = TD.at[0], TD.at[1]

    def dev(x_, y_, z_, c_):
        return (x_ % 2, (x_ // 2) * NY + y_, z_ * 2 + c_)

    rows_sent = [0] * 5

    def send(src, dst, kind, rs, to):
        pltpu.make_async_remote_copy(
            src_ref=src, dst_ref=dst, send_sem=out.at[kind], recv_sem=rs, device_id=to, device_id_type=MESH
        ).start()
        rows_sent[kind] += math.prod(src.shape) // 1024

    def sent(kind):
        rows = rows_sent[kind]
        ref = TD.at[0, pl.ds(0, rows)] if rows <= 1024 else TD.at[:, pl.ds(0, rows // 2)]
        if rows % 16:
            ref = WM.at[pl.ds(0, 8 * rows)]
        pltpu.make_async_remote_copy(
            src_ref=ref, dst_ref=ref, send_sem=out.at[kind], recv_sem=out.at[kind], device_id=mate,
            device_id_type=MESH,
        ).wait_send()

    def arrived(ref, rs):
        pltpu.make_async_remote_copy(
            src_ref=ref, dst_ref=ref, send_sem=rs, recv_sem=rs, device_id=mate, device_id_type=MESH
        ).wait_recv()

    mate = dev(x, y, z, 1 - c)
    yp, ym = dev(x, yr[1], z, c), dev(x, yr[3], z, c)
    xp, xm = dev(xr[1], y, z, c), dev(xr[3], y, z, c)
    zp, zm = dev(x, y, zr[1], c), dev(x, y, zr[7], c)
    xo = xh * 2 + 1 - a
    twin, across = dev(xo, y, z, c), dev(3 - x, y, z, c)
    peers = (
        [mate]
        + [dev(x, yr[k], z, c) for k in (1, 2, 3)]
        + [dev(xr[k], y, z, c) for k in (1, 3)]
        + [dev(x, y, zr[k], c) for k in range(1, NZ)]
        + [dev(xo, yr[k], z, c) for k in (1, 2, 3)]
    )
    barrier = pltpu.get_barrier_semaphore()
    for p in peers:
        pl.semaphore_signal(barrier, inc=1, device_id=p, device_id_type=MESH)

    def block(ref, k, o):
        return ref.at[pl.ds(o * 512 + KPOS[k] * 128, 128)]

    def half(h):
        return pl.ds(pl.multiple_of(h * 512, 512), 512)

    def wpart(x_, rel, r0=0, rows=64):
        return W.at[x_ % 2, POS[rel], pl.ds(r0, rows), half(x_ // 2)]

    def wblock(y_):
        return W.at[a, POS[0], :, pl.ds(pl.multiple_of(xh * 512 + y_ * 128, 128), 128)]

    def wm_rows(y_):
        return WM.at[pl.ds(pl.multiple_of(y_ * 64, 64), 64)]

    own = [
        pltpu.make_async_copy(wu, WU, ls.at[0]),
        pltpu.make_async_copy(wd, WM, ls.at[1]),
        pltpu.make_async_copy(tok, block(TOK, 0, 0), ls.at[2]),
        pltpu.make_async_copy(dy, block(DY, 0, 0), ls.at[3]),
    ]
    for cp in own:
        cp.start()
    own[0].wait()
    own[1].wait()

    @pl.when(a == 0)
    def _():
        WM[...] = WU[...].T

    wblock(y)[...] = wm_rows(y)[...]
    pl.semaphore_wait(barrier, len(peers))

    def first_send():
        for k in (2, 1, 3):
            send(wm_rows(yr[k]), wblock(y), 4, s1r, dev(x, yr[k], z, c))

    def first_done():
        arrived(WM.at[pl.ds(0, 192)], s1r)

    tok0, dy0 = block(TOK, 0, 0), block(DY, 0, 0)

    def tok_up():
        send(tok0, block(TOK, 3, 0), 0, tkr.at[3], yp)

    def tok_down():
        send(tok0, block(TOK, 1, 0), 0, tkr.at[1], ym)

    def dy_up():
        send(dy0, block(DY, 3, 0), 0, dyr.at[3], yp)

    def dy_down():
        send(dy0, block(DY, 1, 0), 0, dyr.at[1], ym)

    def tok_done(k):
        arrived(block(TOK, k, 0), tkr.at[k])

    def dy_done(k):
        arrived(block(DY, k, 0), dyr.at[k])

    def tok_relay():
        tok_done(3)
        send(block(TOK, 3, 0), block(TOK, 2, 0), 0, tkr.at[2], yp)

    def dy_relay():
        dy_done(1)
        send(block(DY, 1, 0), block(DY, 2, 0), 0, dyr.at[2], ym)

    def tok_mate(k):
        send(block(TOK, k, 0), block(TOK, k, 1), 0, mtr.at[k // 2], mate)

    def dy_mate(k):
        send(block(DY, k, 0), block(DY, k, 1), 0, mtr.at[k // 2], mate)

    def mate_done(*ks):
        arrived(TD.at[:, pl.ds(0, 256)], mtr.at[ks[0] // 2])

    def x_send(rel):
        for i, (r0, to) in enumerate(((0, xp), (32, xm), (32, xp), (0, xm))):
            part = wpart(x, rel, r0, 32)
            send(part, part, 1, s3r.at[i, rel] if i < 2 else xdr.at[rel], to)

    def x_up(rel):
        part = wpart(xr[3], rel, 0, 32)
        arrived(part, s3r.at[0, rel])
        send(part, part, 1, xdr.at[rel], xp)

    def x_down(rel):
        part = wpart(xr[1], rel, 32, 32)
        arrived(part, s3r.at[1, rel])
        send(part, part, 1, xdr.at[rel], xm)

    def x_done(rel):
        arrived(W.at[0, POS[rel]], xdr.at[rel])

    nt = (((1,), (1,)), ((), ()))
    tn = (((0,), (0,)), ((), ()))
    nn = (((1,), (0,)), ((), ()))

    def hidden_pass(g, *blocks):
        cols = pl.ds(256 * g, 256)
        up = W[0, 4 * g : 4 * g + 4].reshape(256, 1024)
        down = W[1, 4 * g : 4 * g + 4].reshape(256, 1024)
        for b in blocks:
            rows = pl.ds(256 * b, 256)
            pre = lax.dot_general(TOK[rows, :], up, nt, preferred_element_type=F32)
            hg = lax.dot_general(DY[rows, :], down, nt, preferred_element_type=F32)
            hid, pg = gelu_pair(pre, hg)
            PT[1, cols, rows] = hid.T
            PT[0, cols, rows] = pg.T
            PH[0, rows, cols] = pg

    def z_send(*ks):
        for k in ks:
            send(wpart(x, 0), wpart(x, 8 - k), 1, zrs.at[8 - k], dev(x, y, zr[k], c))

    def z_done(rel):
        arrived(wpart(x, rel), zrs.at[rel])

    def z_done_4():
        arrived(wpart(x, 4), zrs.at[4])

    def z_up():
        z_done(6)
        send(wpart(x, 6), wpart(x, 5), 1, zrs.at[5], zp)
        send(wpart(x, 6, 0, 32), wpart(x, 4, 0, 32), 1, zrs.at[4], dev(x, y, zr[2], c))

    def z_down():
        z_done(2)
        send(wpart(x, 2), wpart(x, 3), 1, zrs.at[3], zm)
        send(wpart(x, 2, 32, 32), wpart(x, 4, 32, 32), 1, zrs.at[4], dev(x, y, zr[6], c))

    def weight_pass(g, i, h):
        left = PT[i, pl.ds(256 * g, 256)]
        grad = lax.dot_general(left, TD[i, :, half(h)], nn, preferred_element_type=F32)
        DWS[i, 4 * g : 4 * g + 4, :, half(h)] = grad.astype(BF16).reshape(4, 64, 512)

    def piece(x_, p, r0=0, rows=64):
        return DWS.at[x_ % 2, p, pl.ds(r0, rows), half(x_ // 2)]

    def add(*refs):
        total = refs[0][...].astype(F32)
        for ref in refs[1:]:
            total = total + ref[...].astype(F32)
        return total.astype(BF16)

    def far_send(p):
        send(piece(xr[2], p, 0, 32), RXA.at[p], 2, rar.at[p], xp)
        send(piece(xr[2], p, 32, 32), RXB.at[p], 2, rbr.at[p], xm)

    def near_send(p):
        send(piece(xr[1], p, 32, 32), RX.at[0, p, pl.ds(32, 32)], 2, xsr.at[p], xp)
        send(piece(xr[3], p, 0, 32), RX.at[1, p, pl.ds(0, 32)], 2, xsr.at[p], xm)

    def x_pass(p):
        arrived(RXA.at[p], rar.at[p])
        SR[p, 0:32] = add(piece(xr[1], p, 0, 32), RXA.at[p])
        send(SR.at[p, pl.ds(0, 32)], RX.at[0, p, pl.ds(0, 32)], 2, xsr.at[p], xp)
        arrived(RXB.at[p], rbr.at[p])
        SR[p, 32:64] = add(piece(xr[3], p, 32, 32), RXB.at[p])
        send(SR.at[p, pl.ds(32, 32)], RX.at[1, p, pl.ds(32, 32)], 2, xsr.at[p], xm)

    def x_sum(p):
        arrived(RX.at[:, p], xsr.at[p])
        SX[p] = add(piece(x, p), RX.at[0, p], RX.at[1, p])

    def z_far_4():
        send(SX.at[0, pl.ds(0, 32)], RZA.at[0], 2, zar.at[0], dev(x, y, zr[2], c))
        send(SX.at[0, pl.ds(32, 32)], RZA.at[1], 2, zar.at[1], dev(x, y, zr[6], c))

    def z_far_up():
        send(SX.at[1], RZB.at[0], 2, zar.at[0], zp)

    def z_far_down():
        send(SX.at[2], RZB.at[1], 2, zar.at[1], zm)

    def z_near(p):
        i = p - 3
        arrived(DXC.at[pl.ds(0, 48)], zar.at[i])
        own_rows, other_rows = pl.ds(32 * i, 32), pl.ds(32 - 32 * i, 32)
        SX[p, own_rows] = add(SX.at[p, own_rows], RZB.at[i, own_rows], RZA.at[i])
        SX[p, other_rows] = add(SX.at[p, other_rows], RZB.at[i, other_rows])
        rel = ORDER[p]
        send(SX.at[p], RZ.at[i], 2, rzr, dev(x, y, zr[rel], c))

    def twin_send(p):
        send(DWS.at[a, p, :, half(1 - xh)], RF.at[p - 5], 2, rfr.at[p - 5], twin)

    def twin_pass(p):
        q = p - 5
        arrived(RF.at[q], rfr.at[q])
        SF[q] = add(DWS.at[1 - a, p, :, half(1 - xh)], RF.at[q])
        send(SF.at[q], RC.at[q], 2, rcr.at[q], across)

    def full_sum(p):
        q = p - 5
        arrived(RC.at[q], rcr.at[q])
        SXF[q] = add(DWS.at[a, p, :, half(xh)], RC.at[q])
        rel = ORDER[p]
        if rel:
            send(SXF.at[q], RZF.at[q], 2, rzr, dev(x, y, zr[rel], c))

    def own_send():
        for i, to in ((0, zp), (1, zm)):
            send(DWS.at[1 - a, 5 + i, :, half(xh)], RZO.at[i], 2, ror, to)

    def dxrows(k):
        return DXS.at[1, pl.ds(KPOS[k] * 128, 128)]

    up_all = W.at[0]

    def dx_rows(i):
        return pl.ds(256 * i, 256)

    def dx_part(rows):
        up = up_all[...].reshape(512, 1024)
        return lax.dot_general(PH[0, rows], up, nn, preferred_element_type=F32)

    def dx_mate(i):
        DXS[0, dx_rows(i)] = dx_part(pl.ds(512 + 256 * i, 256)).astype(BF16)
        send(DXS.at[0, dx_rows(i)], DXC.at[dx_rows(i)], 3, dcr.at[i], mate)

    def dx_own(i):
        ACC[dx_rows(i)] = dx_part(dx_rows(i))

    def dx_pair(i):
        arrived(DXC.at[dx_rows(i)], dcr.at[i])
        DXS[1, dx_rows(i)] = (ACC[dx_rows(i)] + DXC[dx_rows(i)].astype(F32)).astype(BF16)

    def dx_send(*ks):
        for k in ks:
            send(dxrows(k), DXY.at[4 - k], 3, dvr, dev(x, yr[k], z, c))

    def dx_done():
        arrived(DXY.at[pl.ds(1, 3)], dvr)
        DXS[1, 0:128] = add(dxrows(0), DXY.at[1], DXY.at[3], DXY.at[2])
        dx_copy.start()

    dx_copy = pltpu.make_async_copy(dxrows(0), dx_o, ls.at[4])

    def fin(a_, i, y_):
        return gw_o.at[a_, i, pl.ds(pl.multiple_of(y_ * 64, 64), 64)]

    def to_owners(i, *refs):
        total = add(*refs)
        for j in range(NY):
            FS[i, j] = total[:, 128 * j : 128 * (j + 1)]
        for k in (2, 1, 3, 0):
            send(FS.at[i, yr[k]], fin(a, i, y), 3, fr, dev(xo, yr[k], z, c))
        for k in (2, 1, 3):
            send(FS.at[i, yr[k]], fin(a, i, y), 3, fr, dev(x, yr[k], z, c))
        pltpu.make_async_copy(FS.at[i, y], fin(a, i, y), ls.at[5 + i]).start()

    def own_total():
        arrived(RZO, ror)
        to_owners(1, DWS.at[1 - a, 7, :, half(xh)], RZO.at[0], RZO.at[1])

    def total_send():
        arrived(DXC.at[pl.ds(0, 128)], rzr)
        to_owners(0, SXF.at[2], RZF.at[0], RZF.at[1], RZ.at[0], RZ.at[1])

    def total_done():
        arrived(DXC.at[pl.ds(0, 112)], fr)
        for i in (0, 1):
            pltpu.make_async_copy(FS.at[i, y], fin(a, i, y), ls.at[5 + i]).wait()

    first_send()
    own[2].wait()
    own[3].wait()
    tok_up()
    dy_up()
    dy_down()
    first_done()
    z_send(7)
    z_send(2)
    tok_down()
    x_send(0)
    z_send(6)
    z_done(1)
    x_send(1)
    z_up()
    x_send(6)
    dy_relay()
    tok_relay()
    z_down()
    x_send(2)
    z_send(1)
    dy_mate(1)
    z_done(5)
    x_send(5)
    z_done(3)
    x_send(3)
    z_done_4()
    x_send(4)
    x_up(5)
    x_down(5)
    x_down(2)
    x_up(3)
    dy_done(3)
    dy_mate(3)
    x_up(2)
    tok_mate(0)
    dy_mate(0)
    x_down(3)
    x_down(4)
    tok_mate(3)
    x_up(4)
    z_done(7)
    x_send(7)
    x_down(1)
    tok_done(1)
    tok_mate(1)
    dy_done(2)
    dy_mate(2)
    tok_done(2)
    tok_mate(2)
    mate_done(0, 1)
    x_up(6)
    x_down(6)
    x_up(1)
    x_up(0)
    x_done(3)
    x_done(5)
    x_done(2)
    x_down(0)
    x_done(4)
    hidden_pass(0, 1)
    hidden_pass(0, 0)
    x_down(7)
    x_up(7)
    mate_done(3, 2)
    hidden_pass(0, 3)
    hidden_pass(0, 2)
    weight_pass(0, a, 1 - xh)
    far_send(2)
    far_send(0)
    weight_pass(0, 1 - a, 1 - xh)
    far_send(1)
    x_done(6)
    x_done(0)
    x_done(1)
    weight_pass(0, 1 - a, xh)
    near_send(0)
    x_done(7)
    hidden_pass(1, 1)
    far_send(3)
    hidden_pass(1, 0)
    x_pass(2)
    near_send(1)
    hidden_pass(1, 2)
    x_pass(0)
    hidden_pass(1, 3)
    weight_pass(1, a, 1 - xh)
    weight_pass(1, 1 - a, xh)
    twin_send(5)
    own_send()
    far_send(4)
    weight_pass(1, 1 - a, 1 - xh)
    dx_mate(1)
    twin_send(6)
    x_pass(1)
    dx_mate(0)
    near_send(2)
    x_pass(3)
    dx_own(1)
    weight_pass(0, a, xh)
    x_sum(0)
    near_send(4)
    dx_own(0)
    z_far_4()
    dx_pair(0)
    dx_send(1)
    dx_pair(1)
    dx_send(2, 3)
    twin_pass(5)
    weight_pass(1, a, xh)
    near_send(3)
    twin_pass(6)
    x_pass(4)
    x_sum(1)
    z_far_up()
    x_sum(2)
    z_far_down()
    twin_send(7)
    own_total()
    full_sum(5)
    full_sum(6)
    x_sum(3)
    x_sum(4)
    z_near(3)
    z_near(4)
    twin_pass(7)
    full_sum(7)
    total_send()
    dx_done()
    total_done()
    dx_copy.wait()
    for kind in range(5):
        sent(kind)


def finish(dx, gw, dx_o, gu_o, gd_o):
    dx_o[...] = dx[...]
    gu_o[...] = (gw[0, 0].astype(F32) + gw[1, 1].astype(F32)).astype(BF16).T
    gd_o[...] = (gw[1, 0].astype(F32) + gw[0, 1].astype(F32)).astype(BF16)


def shards(tokens, out_grad, w_up, w_down):
    vmem = pl.BlockSpec(memory_space=pltpu.VMEM)
    dma = pltpu.SemaphoreType.DMA
    dx, gw = pl.pallas_call(
        kernel,
        out_shape=(
            jax.ShapeDtypeStruct((128, 1024), BF16),
            jax.ShapeDtypeStruct((2, 2, 256, 128), BF16),
        ),
        in_specs=[pl.BlockSpec(memory_space=pl.ANY)] * 4,
        out_specs=(pl.BlockSpec(memory_space=pl.ANY),) * 2,
        scratch_shapes=[
            pltpu.VMEM((2, 1024, 1024), BF16),
            pltpu.VMEM((2, NZ, 64, 1024), BF16),
            pltpu.VMEM((128, 256), BF16),
            pltpu.VMEM((256, 128), BF16),
            pltpu.VMEM((1, 1024, 512), BF16),
            pltpu.VMEM((2, 512, 1024), BF16),
            pltpu.VMEM((2, NZ, 64, 1024), BF16),
            pltpu.VMEM((5, 32, 512), BF16),
            pltpu.VMEM((5, 32, 512), BF16),
            pltpu.VMEM((2, 5, 64, 512), BF16),
            pltpu.VMEM((5, 64, 512), BF16),
            pltpu.VMEM((5, 64, 512), BF16),
            pltpu.VMEM((2, 32, 512), BF16),
            pltpu.VMEM((2, 64, 512), BF16),
            pltpu.VMEM((2, 64, 512), BF16),
            pltpu.VMEM((3, 64, 512), BF16),
            pltpu.VMEM((3, 64, 512), BF16),
            pltpu.VMEM((3, 64, 512), BF16),
            pltpu.VMEM((3, 64, 512), BF16),
            pltpu.VMEM((2, 64, 512), BF16),
            pltpu.VMEM((2, 64, 512), BF16),
            pltpu.VMEM((2, NY, 64, 128), BF16),
            pltpu.VMEM((512, 1024), F32),
            pltpu.VMEM((2, 512, 1024), BF16),
            pltpu.VMEM((512, 1024), BF16),
            pltpu.VMEM((NY, 128, 1024), BF16),
            dma((7,)), dma((5,)), dma,
            dma((NY,)), dma((NY,)), dma((2,)),
            dma((NZ,)), dma((2, NZ)), dma((NZ,)),
            dma((5,)), dma((5,)), dma((5,)),
            dma((3,)), dma((3,)), dma((2,)), dma, dma, dma,
            dma((2,)), dma,
        ],
        compiler_params=pltpu.CompilerParams(
            collective_id=0, has_side_effects=True, vmem_limit_bytes=56 << 20
        ),
        cost_estimate=pl.CostEstimate(
            flops=5 * 2 * 1024 * 512 * 1024, bytes_accessed=2 << 20, transcendentals=1024 * 512
        ),
        name="mlp_backward",
    )(tokens, out_grad, w_up, w_down)
    return pl.pallas_call(
        finish,
        out_shape=(
            jax.ShapeDtypeStruct((128, 1024), BF16),
            jax.ShapeDtypeStruct((128, 256), BF16),
            jax.ShapeDtypeStruct((256, 128), BF16),
        ),
        in_specs=[vmem] * 2,
        out_specs=(vmem,) * 3,
        name="finish",
    )(dx, gw)


def solution(mesh):
    return jax.shard_map(
        shards,
        mesh=mesh,
        in_specs=(
            P(("dp", "row", "col"), None),
            P(("dp", "row", "col"), None),
            P("row", "col"),
            P("col", "row"),
        ),
        out_specs=(P(("dp", "row", "col"), None), P("row", "col"), P("col", "row")),
        check_vma=False,
    )
```

```python
import math

import jax
import jax.numpy as jnp
from jax import lax
from jax.experimental import pallas as pl
from jax.experimental.pallas import tpu as pltpu
from jax.sharding import PartitionSpec as P

MESH = pl.DeviceIdType.MESH
BF16 = jnp.bfloat16
F32 = jnp.float32
NX, NY, NZ = 4, 4, 8
ORDER = (4, 3, 5, 2, 6, 1, 7, 0)
KPOS = (0, 1, 3, 2)
POS = [ORDER.index(rel) for rel in range(NZ)]


def gelu_pair(pre, hid_grad):
    k = 0.7978845608028654
    sq = pre * pre
    t = jnp.tanh(pre * (k + (k * 0.044715) * sq))
    half = 0.5 * (1.0 + t)
    hidden = pre * half
    slope = half + (0.5 * pre) * (1.0 - t * t) * (k + (3.0 * k * 0.044715) * sq)
    return hidden.astype(BF16), (hid_grad * slope).astype(BF16)


def kernel(
    tok, dy, wu, wd, dx_o, gw_o,
    TD, W, WU, WM, PH, PT, DWS, RXA, RXB, RX, SR, SX, RZA, RZB, RZ, RF, SF, RC, SXF, RZF, RZO, FS, ACC, DXS, DXC, DXY,
    ls, out, s1r, tkr, dyr, mtr, zrs, s3r, xdr, rar, rbr, xsr, rfr, rcr, zar, rzr, ror, fr, dcr, dvr,
):
    a = lax.axis_index("dp")
    row = lax.axis_index("row")
    col = lax.axis_index("col")
    xh, y = row // NY, row % NY
    z, c = col // 2, col % 2
    x = xh * 2 + a
    xr = [x, (x + 1) % NX, (x + 2) % NX, (x + 3) % NX]
    yr = [y, (y + 1) % NY, (y + 2) % NY, (y + 3) % NY]
    zr = [(z + k) % NZ for k in range(NZ)]
    TOK, DY = TD.at[0], TD.at[1]

    def dev(x_, y_, z_, c_):
        return (x_ % 2, (x_ // 2) * NY + y_, z_ * 2 + c_)

    rows_sent = [0] * 5

    def send(src, dst, kind, rs, to):
        pltpu.make_async_remote_copy(
            src_ref=src, dst_ref=dst, send_sem=out.at[kind], recv_sem=rs, device_id=to, device_id_type=MESH
        ).start()
        rows_sent[kind] += math.prod(src.shape) // 1024

    def sent(kind):
        rows = rows_sent[kind]
        ref = TD.at[0, pl.ds(0, rows)] if rows <= 1024 else TD.at[:, pl.ds(0, rows // 2)]
        if rows % 16:
            ref = WM.at[pl.ds(0, 8 * rows)]
        pltpu.make_async_remote_copy(
            src_ref=ref, dst_ref=ref, send_sem=out.at[kind], recv_sem=out.at[kind], device_id=mate,
            device_id_type=MESH,
        ).wait_send()

    def arrived(ref, rs):
        pltpu.make_async_remote_copy(
            src_ref=ref, dst_ref=ref, send_sem=rs, recv_sem=rs, device_id=mate, device_id_type=MESH
        ).wait_recv()

    mate = dev(x, y, z, 1 - c)
    yp, ym = dev(x, yr[1], z, c), dev(x, yr[3], z, c)
    xp, xm = dev(xr[1], y, z, c), dev(xr[3], y, z, c)
    zp, zm = dev(x, y, zr[1], c), dev(x, y, zr[7], c)
    xo = xh * 2 + 1 - a
    twin, across = dev(xo, y, z, c), dev(3 - x, y, z, c)
    peers = (
        [mate]
        + [dev(x, yr[k], z, c) for k in (1, 2, 3)]
        + [dev(xr[k], y, z, c) for k in (1, 3)]
        + [dev(x, y, zr[k], c) for k in range(1, NZ)]
        + [dev(xo, yr[k], z, c) for k in (1, 2, 3)]
    )
    barrier = pltpu.get_barrier_semaphore()
    for p in peers:
        pl.semaphore_signal(barrier, inc=1, device_id=p, device_id_type=MESH)

    def block(ref, k, o):
        return ref.at[pl.ds(o * 512 + KPOS[k] * 128, 128)]

    def half(h):
        return pl.ds(pl.multiple_of(h * 512, 512), 512)

    def wpart(x_, rel, r0=0, rows=64):
        return W.at[x_ % 2, POS[rel], pl.ds(r0, rows), half(x_ // 2)]

    def wblock(y_):
        return W.at[a, POS[0], :, pl.ds(pl.multiple_of(xh * 512 + y_ * 128, 128), 128)]

    def wm_rows(y_):
        return WM.at[pl.ds(pl.multiple_of(y_ * 64, 64), 64)]

    own = [
        pltpu.make_async_copy(wu, WU, ls.at[0]),
        pltpu.make_async_copy(wd, WM, ls.at[1]),
        pltpu.make_async_copy(tok, block(TOK, 0, 0), ls.at[2]),
        pltpu.make_async_copy(dy, block(DY, 0, 0), ls.at[3]),
    ]
    for cp in own:
        cp.start()
    own[0].wait()
    own[1].wait()

    @pl.when(a == 0)
    def _():
        WM[...] = WU[...].T

    wblock(y)[...] = wm_rows(y)[...]
    pl.semaphore_wait(barrier, len(peers))

    def first_send():
        for k in (2, 1, 3):
            send(wm_rows(yr[k]), wblock(y), 4, s1r, dev(x, yr[k], z, c))

    def first_done():
        arrived(WM.at[pl.ds(0, 192)], s1r)

    tok0, dy0 = block(TOK, 0, 0), block(DY, 0, 0)

    def tok_up():
        send(tok0, block(TOK, 3, 0), 0, tkr.at[3], yp)

    def tok_down():
        send(tok0, block(TOK, 1, 0), 0, tkr.at[1], ym)

    def dy_up():
        send(dy0, block(DY, 3, 0), 0, dyr.at[3], yp)

    def dy_down():
        send(dy0, block(DY, 1, 0), 0, dyr.at[1], ym)

    def tok_done(k):
        arrived(block(TOK, k, 0), tkr.at[k])

    def dy_done(k):
        arrived(block(DY, k, 0), dyr.at[k])

    def tok_relay():
        tok_done(3)
        send(block(TOK, 3, 0), block(TOK, 2, 0), 0, tkr.at[2], yp)

    def dy_relay():
        dy_done(1)
        send(block(DY, 1, 0), block(DY, 2, 0), 0, dyr.at[2], ym)

    def tok_mate(k):
        send(block(TOK, k, 0), block(TOK, k, 1), 0, mtr.at[k // 2], mate)

    def dy_mate(k):
        send(block(DY, k, 0), block(DY, k, 1), 0, mtr.at[k // 2], mate)

    def mate_done(*ks):
        arrived(TD.at[:, pl.ds(0, 256)], mtr.at[ks[0] // 2])

    def x_send(rel):
        for i, (r0, to) in enumerate(((0, xp), (32, xm), (32, xp), (0, xm))):
            part = wpart(x, rel, r0, 32)
            send(part, part, 1, s3r.at[i, rel] if i < 2 else xdr.at[rel], to)

    def x_up(rel):
        part = wpart(xr[3], rel, 0, 32)
        arrived(part, s3r.at[0, rel])
        send(part, part, 1, xdr.at[rel], xp)

    def x_down(rel):
        part = wpart(xr[1], rel, 32, 32)
        arrived(part, s3r.at[1, rel])
        send(part, part, 1, xdr.at[rel], xm)

    def x_done(rel):
        arrived(W.at[0, POS[rel]], xdr.at[rel])

    nt = (((1,), (1,)), ((), ()))
    tn = (((0,), (0,)), ((), ()))
    nn = (((1,), (0,)), ((), ()))

    def hidden_pass(g, *blocks):
        cols = pl.ds(256 * g, 256)
        up = W[0, 4 * g : 4 * g + 4].reshape(256, 1024)
        down = W[1, 4 * g : 4 * g + 4].reshape(256, 1024)
        for b in blocks:
            rows = pl.ds(256 * b, 256)
            pre = lax.dot_general(TOK[rows, :], up, nt, preferred_element_type=F32)
            hg = lax.dot_general(DY[rows, :], down, nt, preferred_element_type=F32)
            hid, pg = gelu_pair(pre, hg)
            PT[1, cols, rows] = hid.T
            PT[0, cols, rows] = pg.T
            PH[0, rows, cols] = pg

    def z_send(*ks):
        for k in ks:
            send(wpart(x, 0), wpart(x, 8 - k), 1, zrs.at[8 - k], dev(x, y, zr[k], c))

    def z_done(rel):
        arrived(wpart(x, rel), zrs.at[rel])

    def z_done_4():
        arrived(wpart(x, 4), zrs.at[4])

    def z_up():
        z_done(6)
        send(wpart(x, 6), wpart(x, 5), 1, zrs.at[5], zp)
        send(wpart(x, 6, 0, 32), wpart(x, 4, 0, 32), 1, zrs.at[4], dev(x, y, zr[2], c))

    def z_down():
        z_done(2)
        send(wpart(x, 2), wpart(x, 3), 1, zrs.at[3], zm)
        send(wpart(x, 2, 32, 32), wpart(x, 4, 32, 32), 1, zrs.at[4], dev(x, y, zr[6], c))

    def weight_pass(g, i, h):
        left = PT[i, pl.ds(256 * g, 256)]
        grad = lax.dot_general(left, TD[i, :, half(h)], nn, preferred_element_type=F32)
        DWS[i, 4 * g : 4 * g + 4, :, half(h)] = grad.astype(BF16).reshape(4, 64, 512)

    def piece(x_, p, r0=0, rows=64):
        return DWS.at[x_ % 2, p, pl.ds(r0, rows), half(x_ // 2)]

    def add(*refs):
        total = refs[0][...].astype(F32)
        for ref in refs[1:]:
            total = total + ref[...].astype(F32)
        return total.astype(BF16)

    def far_send(p):
        send(piece(xr[2], p, 0, 32), RXA.at[p], 2, rar.at[p], xp)
        send(piece(xr[2], p, 32, 32), RXB.at[p], 2, rbr.at[p], xm)

    def near_send(p):
        send(piece(xr[1], p, 32, 32), RX.at[0, p, pl.ds(32, 32)], 2, xsr.at[p], xp)
        send(piece(xr[3], p, 0, 32), RX.at[1, p, pl.ds(0, 32)], 2, xsr.at[p], xm)

    def x_pass(p):
        arrived(RXA.at[p], rar.at[p])
        SR[p, 0:32] = add(piece(xr[1], p, 0, 32), RXA.at[p])
        send(SR.at[p, pl.ds(0, 32)], RX.at[0, p, pl.ds(0, 32)], 2, xsr.at[p], xp)
        arrived(RXB.at[p], rbr.at[p])
        SR[p, 32:64] = add(piece(xr[3], p, 32, 32), RXB.at[p])
        send(SR.at[p, pl.ds(32, 32)], RX.at[1, p, pl.ds(32, 32)], 2, xsr.at[p], xm)

    def x_sum(p):
        arrived(RX.at[:, p], xsr.at[p])
        SX[p] = add(piece(x, p), RX.at[0, p], RX.at[1, p])

    def z_far_4():
        send(SX.at[0, pl.ds(0, 32)], RZA.at[0], 2, zar.at[0], dev(x, y, zr[2], c))
        send(SX.at[0, pl.ds(32, 32)], RZA.at[1], 2, zar.at[1], dev(x, y, zr[6], c))

    def z_far_up():
        send(SX.at[1], RZB.at[0], 2, zar.at[0], zp)

    def z_far_down():
        send(SX.at[2], RZB.at[1], 2, zar.at[1], zm)

    def z_near(p):
        i = p - 3
        arrived(DXC.at[pl.ds(0, 48)], zar.at[i])
        own_rows, other_rows = pl.ds(32 * i, 32), pl.ds(32 - 32 * i, 32)
        SX[p, own_rows] = add(SX.at[p, own_rows], RZB.at[i, own_rows], RZA.at[i])
        SX[p, other_rows] = add(SX.at[p, other_rows], RZB.at[i, other_rows])
        rel = ORDER[p]
        send(SX.at[p], RZ.at[i], 2, rzr, dev(x, y, zr[rel], c))

    def twin_send(p):
        send(DWS.at[a, p, :, half(1 - xh)], RF.at[p - 5], 2, rfr.at[p - 5], twin)

    def twin_pass(p):
        q = p - 5
        arrived(RF.at[q], rfr.at[q])
        SF[q] = add(DWS.at[1 - a, p, :, half(1 - xh)], RF.at[q])
        send(SF.at[q], RC.at[q], 2, rcr.at[q], across)

    def full_sum(p):
        q = p - 5
        arrived(RC.at[q], rcr.at[q])
        SXF[q] = add(DWS.at[a, p, :, half(xh)], RC.at[q])
        rel = ORDER[p]
        if rel:
            send(SXF.at[q], RZF.at[q], 2, rzr, dev(x, y, zr[rel], c))

    def own_send():
        for i, to in ((0, zp), (1, zm)):
            send(DWS.at[1 - a, 5 + i, :, half(xh)], RZO.at[i], 2, ror, to)

    def dxrows(k):
        return DXS.at[1, pl.ds(KPOS[k] * 128, 128)]

    up_all = W.at[0]

    def dx_rows(i):
        return pl.ds(256 * i, 256)

    def dx_part(rows):
        up = up_all[...].reshape(512, 1024)
        return lax.dot_general(PH[0, rows], up, nn, preferred_element_type=F32)

    def dx_mate(i):
        DXS[0, dx_rows(i)] = dx_part(pl.ds(512 + 256 * i, 256)).astype(BF16)
        send(DXS.at[0, dx_rows(i)], DXC.at[dx_rows(i)], 3, dcr.at[i], mate)

    def dx_own(i):
        ACC[dx_rows(i)] = dx_part(dx_rows(i))

    def dx_pair(i):
        arrived(DXC.at[dx_rows(i)], dcr.at[i])
        DXS[1, dx_rows(i)] = (ACC[dx_rows(i)] + DXC[dx_rows(i)].astype(F32)).astype(BF16)

    def dx_send(*ks):
        for k in ks:
            send(dxrows(k), DXY.at[4 - k], 3, dvr, dev(x, yr[k], z, c))

    def dx_done():
        arrived(DXY.at[pl.ds(1, 3)], dvr)
        DXS[1, 0:128] = add(dxrows(0), DXY.at[1], DXY.at[3], DXY.at[2])
        dx_copy.start()

    dx_copy = pltpu.make_async_copy(dxrows(0), dx_o, ls.at[4])

    def fin(a_, i, y_):
        return gw_o.at[a_, i, pl.ds(pl.multiple_of(y_ * 64, 64), 64)]

    def to_owners(i, *refs):
        total = add(*refs)
        for j in range(NY):
            FS[i, j] = total[:, 128 * j : 128 * (j + 1)]
        for k in (2, 1, 3, 0):
            send(FS.at[i, yr[k]], fin(a, i, y), 3, fr, dev(xo, yr[k], z, c))
        for k in (2, 1, 3):
            send(FS.at[i, yr[k]], fin(a, i, y), 3, fr, dev(x, yr[k], z, c))
        pltpu.make_async_copy(FS.at[i, y], fin(a, i, y), ls.at[5 + i]).start()

    def own_total():
        arrived(RZO, ror)
        to_owners(1, DWS.at[1 - a, 7, :, half(xh)], RZO.at[0], RZO.at[1])

    def total_send():
        arrived(DXC.at[pl.ds(0, 128)], rzr)
        to_owners(0, SXF.at[2], RZF.at[0], RZF.at[1], RZ.at[0], RZ.at[1])

    def total_done():
        arrived(DXC.at[pl.ds(0, 112)], fr)
        for i in (0, 1):
            pltpu.make_async_copy(FS.at[i, y], fin(a, i, y), ls.at[5 + i]).wait()

    first_send()
    own[2].wait()
    own[3].wait()
    tok_up()
    dy_down()
    tok_down()
    first_done()
    z_send(7)
    z_send(2)
    z_send(6)
    x_send(0)
    x_down(0)
    x_up(0)
    dy_up()
    z_done(1)
    x_send(1)
    z_up()
    x_send(6)
    dy_relay()
    z_send(1)
    z_down()
    x_send(2)
    tok_relay()
    z_done(5)
    x_send(5)
    tok_mate(0)
    dy_mate(0)
    z_done(3)
    x_send(3)
    z_done_4()
    x_send(4)
    x_up(2)
    x_down(5)
    x_down(3)
    x_down(2)
    x_up(5)
    x_up(3)
    dy_mate(1)
    x_down(4)
    dy_done(3)
    dy_mate(3)
    x_up(4)
    tok_done(1)
    tok_mate(1)
    z_done(7)
    x_send(7)
    x_down(6)
    tok_mate(3)
    x_done(5)
    x_up(6)
    dy_done(2)
    dy_mate(2)
    x_done(3)
    mate_done(0, 1)
    tok_done(2)
    tok_mate(2)
    x_down(1)
    x_up(1)
    x_done(2)
    x_done(4)
    hidden_pass(0, 0)
    hidden_pass(0, 2)
    hidden_pass(0, 1)
    x_up(7)
    x_down(7)
    mate_done(3, 2)
    hidden_pass(0, 3)
    weight_pass(0, a, 1 - xh)
    far_send(1)
    far_send(0)
    weight_pass(0, 1 - a, xh)
    x_done(0)
    weight_pass(0, 1 - a, 1 - xh)
    near_send(0)
    far_send(3)
    near_send(1)
    x_done(6)
    far_send(2)
    x_done(1)
    x_done(7)
    hidden_pass(1, 3)
    dx_mate(1)
    hidden_pass(1, 0)
    hidden_pass(1, 1)
    x_pass(0)
    hidden_pass(1, 2)
    weight_pass(1, a, 1 - xh)
    far_send(4)
    weight_pass(1, 1 - a, xh)
    twin_send(6)
    x_pass(1)
    near_send(2)
    own_send()
    dx_own(0)
    x_pass(2)
    weight_pass(0, a, xh)
    weight_pass(1, 1 - a, 1 - xh)
    x_sum(0)
    dx_own(1)
    z_far_4()
    twin_send(5)
    near_send(3)
    dx_mate(0)
    x_pass(3)
    near_send(4)
    dx_pair(1)
    dx_send(2, 3)
    twin_pass(6)
    weight_pass(1, a, xh)
    x_sum(1)
    z_far_up()
    x_pass(4)
    twin_send(7)
    x_sum(2)
    z_far_down()
    twin_pass(5)
    own_total()
    full_sum(6)
    x_sum(3)
    z_near(3)
    dx_pair(0)
    dx_send(1)
    x_sum(4)
    z_near(4)
    twin_pass(7)
    full_sum(5)
    full_sum(7)
    total_send()
    dx_done()
    total_done()
    dx_copy.wait()
    for kind in range(5):
        sent(kind)


def finish(dx, gw, dx_o, gu_o, gd_o):
    dx_o[...] = dx[...]
    gu_o[...] = (gw[0, 0].astype(F32) + gw[1, 1].astype(F32)).astype(BF16).T
    gd_o[...] = (gw[1, 0].astype(F32) + gw[0, 1].astype(F32)).astype(BF16)


def shards(tokens, out_grad, w_up, w_down):
    vmem = pl.BlockSpec(memory_space=pltpu.VMEM)
    dma = pltpu.SemaphoreType.DMA
    dx, gw = pl.pallas_call(
        kernel,
        out_shape=(
            jax.ShapeDtypeStruct((128, 1024), BF16),
            jax.ShapeDtypeStruct((2, 2, 256, 128), BF16),
        ),
        in_specs=[pl.BlockSpec(memory_space=pl.ANY)] * 4,
        out_specs=(pl.BlockSpec(memory_space=pl.ANY),) * 2,
        scratch_shapes=[
            pltpu.VMEM((2, 1024, 1024), BF16),
            pltpu.VMEM((2, NZ, 64, 1024), BF16),
            pltpu.VMEM((128, 256), BF16),
            pltpu.VMEM((256, 128), BF16),
            pltpu.VMEM((1, 1024, 512), BF16),
            pltpu.VMEM((2, 512, 1024), BF16),
            pltpu.VMEM((2, NZ, 64, 1024), BF16),
            pltpu.VMEM((5, 32, 512), BF16),
            pltpu.VMEM((5, 32, 512), BF16),
            pltpu.VMEM((2, 5, 64, 512), BF16),
            pltpu.VMEM((5, 64, 512), BF16),
            pltpu.VMEM((5, 64, 512), BF16),
            pltpu.VMEM((2, 32, 512), BF16),
            pltpu.VMEM((2, 64, 512), BF16),
            pltpu.VMEM((2, 64, 512), BF16),
            pltpu.VMEM((3, 64, 512), BF16),
            pltpu.VMEM((3, 64, 512), BF16),
            pltpu.VMEM((3, 64, 512), BF16),
            pltpu.VMEM((3, 64, 512), BF16),
            pltpu.VMEM((2, 64, 512), BF16),
            pltpu.VMEM((2, 64, 512), BF16),
            pltpu.VMEM((2, NY, 64, 128), BF16),
            pltpu.VMEM((512, 1024), F32),
            pltpu.VMEM((2, 512, 1024), BF16),
            pltpu.VMEM((512, 1024), BF16),
            pltpu.VMEM((NY, 128, 1024), BF16),
            dma((7,)), dma((5,)), dma,
            dma((NY,)), dma((NY,)), dma((2,)),
            dma((NZ,)), dma((2, NZ)), dma((NZ,)),
            dma((5,)), dma((5,)), dma((5,)),
            dma((3,)), dma((3,)), dma((2,)), dma, dma, dma,
            dma((2,)), dma,
        ],
        compiler_params=pltpu.CompilerParams(
            collective_id=0, has_side_effects=True, vmem_limit_bytes=56 << 20
        ),
        cost_estimate=pl.CostEstimate(
            flops=5 * 2 * 1024 * 512 * 1024, bytes_accessed=2 << 20, transcendentals=1024 * 512
        ),
        name="mlp_backward",
    )(tokens, out_grad, w_up, w_down)
    return pl.pallas_call(
        finish,
        out_shape=(
            jax.ShapeDtypeStruct((128, 1024), BF16),
            jax.ShapeDtypeStruct((128, 256), BF16),
            jax.ShapeDtypeStruct((256, 128), BF16),
        ),
        in_specs=[vmem] * 2,
        out_specs=(vmem,) * 3,
        name="finish",
    )(dx, gw)


def solution(mesh):
    return jax.shard_map(
        shards,
        mesh=mesh,
        in_specs=(
            P(("dp", "row", "col"), None),
            P(("dp", "row", "col"), None),
            P("row", "col"),
            P("col", "row"),
        ),
        out_specs=(P(("dp", "row", "col"), None), P("row", "col"), P("col", "row")),
        check_vma=False,
    )
```
